256 devices in a mesh: row: 16 (over z_hi, x), col: 16 (over y, z_lo, core).
Axes of the slice: x: 4, y: 4, z: 8 (z_hi: 4, z_lo: 2; z = z_hi * 2 + z_lo), core: 2. Of those that a mesh axis runs over, the one named last changes fastest.
Arguments:
- object_field: float32 [2, 8192, 8192], P(None, 'row', 'col'), may hold values from -5 to 5
- probe_modes: float32 [4, 2, 128, 128], replicated, may hold values from -5 to 5
- amplitudes: float32 [16, 16, 16, 128, 128], P('row', 'col'), may hold values from 0.5 to 2
- offsets: int32 [16, 16, 16, 2], P('row', 'col'), may hold values from -64 to 447
- counts: int32 [16, 16], P('row', 'col'), may hold values from 1 to 16, as said below
Outputs:
- object_grad: float32 [2, 8192, 8192], P(None, 'row', 'col')
- probe_grad: float32 [4, 2, 128, 128], replicated
The draws below stay inside these ranges and needn't reach their ends.
Inputs may be any that keep to these rules, and one draw needn't show every extreme that they name: `counts`: live slots come first on each device; some device is full in every draw.
All inputs are finite; a program needn't handle non-finite values.
Results may differ from the reference program's by a relative error of at most 0.0001.
Values sent between devices are 32-bit elements; how exact they have to be, the bound alone decides.
No kernel may reach another device: no remote copies, remote signals or barrier semaphores. Data moves between devices by JAX's collectives and lax.ppermute only.
A program may use at most 64 MiB of HBM per device.

```python
import math
import jax
import jax.numpy as jnp
from jax import lax

PATCH = 128
MODES = 4
TILE = 512
POS_DEV = 16
HALO = 64
ROWS = 8192
COLS = 8192
N_ROW = 16
N_COL = 16


def draw_counts(key, part):
    key = jax.random.fold_in(key, 7)
    first_key, second_key = jax.random.split(key)
    device_loads = jax.random.randint(first_key, (N_ROW * N_COL,), 1, POS_DEV // 2 + 1)
    heavy_picks = jax.random.randint(second_key, (max(1, N_ROW * N_COL // 16),), 0, N_ROW * N_COL)
    device_loads = device_loads.at[heavy_picks].set(POS_DEV)
    return device_loads.reshape(N_ROW, N_COL).astype(jnp.int32)


def set_ends(entries, key, least, largest):
    spot = [jax.random.randint(jax.random.fold_in(key, axis), (), 0, length) for axis, length in enumerate(entries.shape)]
    widest = entries.shape.index(max(entries.shape))
    beside = spot[:widest] + [(spot[widest] + 1) % entries.shape[widest]] + spot[widest + 1:]
    return entries.at[tuple(spot)].set(least).at[tuple(beside)].set(largest)


def steps_of(key, extent, cuts, low, high):
    def one(dim, blocks):
        draws = jax.random.uniform(jax.random.fold_in(jax.random.fold_in(key, 6), dim), (blocks,), jnp.float32, low / len(cuts), high / len(cuts))
        return jnp.repeat(jnp.exp(draws), extent[dim] // blocks).reshape((-1,) + (1,) * (len(extent) - dim - 1))

    level = one(*cuts[0])
    for cut in cuts[1:]:
        level = level * one(*cut)
    return level


def scatter_about(own_key, extent, scale, reach, shards=(), held_as=jnp.bfloat16):
    drawn = jax.random.normal(own_key, extent, jnp.float32) * scale
    if len(shards) > 0:
        drawn = steps_of(own_key, extent, shards, -0.22, 0.18) * drawn
    return jnp.clip(drawn, min=-reach, max=reach).astype(held_as)


def setup_inputs(seed: int = 0) -> dict:
    keys = jax.random.split(jax.random.key(seed), 6)
    object_field = scatter_about(keys[0], (2, ROWS, COLS), 0.7, 5.0, ((1, 16), (2, 16)), jnp.float32)
    probe_modes = scatter_about(keys[1], (MODES, 2, PATCH, PATCH), 0.7, 5.0, (), jnp.float32)
    amplitudes = jnp.clip(0.5 + 1.5 * jax.random.uniform(keys[2], (N_ROW, N_COL, POS_DEV, PATCH, PATCH), jnp.float32) ** steps_of(keys[2], (N_ROW, N_COL, POS_DEV, PATCH, PATCH), ((0, 16), (1, 16)), -0.2, 0.2), 0.5, 2.0)
    offsets = set_ends(jax.random.randint(keys[3], (N_ROW, N_COL, POS_DEV, 2), -HALO, TILE - HALO), jax.random.fold_in(keys[3], 1), -HALO, (TILE - HALO) - 1).astype(jnp.int32)
    counts = draw_counts(jax.random.fold_in(keys[5], 71), 0)
    return dict(object_field=object_field, probe_modes=probe_modes, amplitudes=amplitudes, offsets=offsets, counts=counts)


def reference(object_field, probe_modes, amplitudes, offsets, counts):
    half_width = PATCH // 2
    whole = lax.complex(object_field[0], object_field[1])
    padded = jnp.pad(whole, half_width)
    probe = lax.complex(probe_modes[:, 0], probe_modes[:, 1])
    tile_rows = jnp.arange(N_ROW, dtype=jnp.int32)[:, None, None] * TILE
    tile_cols = jnp.arange(N_COL, dtype=jnp.int32)[None, :, None] * TILE
    tops = (tile_rows + offsets[..., 0] + half_width).astype(jnp.int32).reshape(-1)
    lefts = (tile_cols + offsets[..., 1] + half_width).astype(jnp.int32).reshape(-1)
    lives = (jnp.arange(POS_DEV, dtype=jnp.int32)[None, None, :] < counts[:, :, None]).reshape(-1)
    measured = amplitudes.reshape(-1, PATCH, PATCH)

    def advance(totals, record):
        object_total, probe_total = totals
        amplitude, top_at, left_at, live_flag = record
        patch = lax.dynamic_slice(padded, (top_at, left_at), (PATCH, PATCH))
        far_field = jnp.fft.fft2(probe * patch[None], norm='ortho')
        intensity = lax.optimization_barrier(jnp.sum(jnp.real(far_field) ** 2 + jnp.imag(far_field) ** 2, axis=0))
        residual = jnp.where(live_flag, intensity - amplitude * amplitude, 0.0)
        returned = jnp.fft.ifft2(2.0 * residual[None] * far_field, norm='ortho')
        patch_grad = lax.optimization_barrier(jnp.sum(jnp.conj(probe) * returned, axis=0))
        current = lax.dynamic_slice(object_total, (top_at, left_at), (PATCH, PATCH))
        object_total = lax.dynamic_update_slice(object_total, current + patch_grad, (top_at, left_at))
        probe_total = probe_total + jnp.conj(patch)[None] * returned
        return ((object_total, probe_total), None)
    start_state = (jnp.zeros_like(padded), jnp.zeros_like(probe))
    (object_total, probe_total), _ = lax.scan(advance, start_state, (measured, tops, lefts, lives))
    inner = object_total[half_width:-half_width, half_width:-half_width]
    object_grad = jnp.stack([jnp.real(inner), jnp.imag(inner)]).astype(jnp.float32)
    factor = 1.0 / math.sqrt(N_ROW * N_COL * POS_DEV)
    probe_grad = (jnp.stack([jnp.real(probe_total), jnp.imag(probe_total)], axis=1) * factor).astype(jnp.float32)
    return (object_grad, probe_grad)
```

```python
import functools
import math

import jax
import jax.numpy as jnp
import ml_dtypes
import numpy as np
from jax import lax
from jax.experimental import pallas as pl
from jax.experimental.pallas import tpu as pltpu
from jax.sharding import Mesh
from jax.sharding import PartitionSpec as P

PATCH = 128
MODES = 4
TILE = 512
SLOTS = 16
HALF = 64
EXT = TILE + 2 * HALF
BLOCKS = 6
UNROLL = 2

ROW = ("zh", "x")
COL = ("y", "zl", "core")


def split_table(table):
    high = table.astype(np.float32).astype(ml_dtypes.bfloat16)
    low = (table - high.astype(np.float64)).astype(np.float32).astype(ml_dtypes.bfloat16)
    return high, low


def dft_tables(n):
    i = np.arange(n)
    angles = (np.outer(i, i) % n) * (2 * math.pi / n)
    cos, sin = np.cos(angles) / math.sqrt(n), -np.sin(angles) / math.sqrt(n)
    forward = np.block([[cos, sin], [-sin, cos]])
    fh, fl = split_table(forward)
    ih, il = split_table(forward.T)
    return (
        np.concatenate([fh, fh, fl], 0),
        np.concatenate([ih, il, ih], 1),
        np.concatenate([fh, fl, fh], 1),
        np.concatenate([ih, ih, il], 0),
    )


def split(x):
    high = x.astype(jnp.bfloat16)
    return high, (x - high.astype(jnp.float32)).astype(jnp.bfloat16)


def dot(a, b):
    return jnp.dot(a, b, preferred_element_type=jnp.float32)


def right_dft(x, table):
    high, low = split(x)
    return dot(jnp.concatenate([high, low, high], 1), table)


def left_dft(table, x):
    high, low = split(x)
    return dot(table, jnp.concatenate([high, high, low], 0))


def to_cols(y):
    n = PATCH
    return jnp.concatenate(
        [jnp.concatenate([y[m * n : (m + 1) * n, p * n : (p + 1) * n] for m in range(MODES)], 1) for p in range(2)], 0
    )


def to_rows(z):
    n = PATCH
    return jnp.concatenate(
        [jnp.concatenate([z[p * n : (p + 1) * n, m * n : (m + 1) * n] for p in range(2)], 1) for m in range(MODES)], 0
    )


def lane_iota(rows):
    return lax.broadcasted_iota(jnp.int32, (rows, PATCH), 1)


def is_inside(offsets, k):
    r, c = offsets[2 * k], offsets[2 * k + 1]
    top = TILE - PATCH
    return (r >= 0) & (r <= top) & (c >= 0) & (c <= top)


def early_slots(counts, offsets):
    live = counts[0]

    def tally(k, total):
        return total + jnp.where(is_inside(offsets, k) & (k < live), 1, 0)

    inside = lax.fori_loop(0, SLOTS, tally, 0)
    return live, inside // UNROLL * UNROLL


def choose_slots(counts, offsets, chosen, early):
    live, first = early_slots(counts, offsets)

    def pick(k, state):
        seen, size = state
        inner = is_inside(offsets, k)
        is_early = inner & (seen < first)
        chosen[size] = k
        take = (is_early == early) & (k < live)
        seen = seen + jnp.where(inner, 1, 0)
        return seen, size + jnp.where(take, 1, 0)

    _, size = lax.fori_loop(0, SLOTS, pick, (0, 0))
    return size


def slot_work(k, out_slot, scale, offsets, extended, amplitudes, probe, tables, patch_grads, probe_total):
    rf, lf, li, ri = tables
    n = PATCH
    row = offsets[2 * k] + HALF
    col = offsets[2 * k + 1] + PATCH
    block = col // n
    lead = col - block * n
    turn = jnp.where(lead == 0, 0, n - lead)
    lane = lane_iota(n)
    parts = []
    for p in range(2):
        a = pltpu.roll(extended[p, block, pl.ds(row, n), :], turn, 1)
        b = pltpu.roll(extended[p, block + 1, pl.ds(row, n), :], turn, 1)
        parts.append(jnp.where(lane < n - lead, a, b))
    obj_r, obj_i = parts
    waves = []
    for m in range(MODES):
        pr, pi = probe[m, 0], probe[m, 1]
        waves.append(jnp.concatenate([pr * obj_r - pi * obj_i, pr * obj_i + pi * obj_r], 1))
    far = left_dft(lf[...], to_cols(right_dft(jnp.concatenate(waves, 0), rf[...])))
    power = far * far
    power = power[:n] + power[n:]
    intensity = power[:, :n] + power[:, n : 2 * n] + power[:, 2 * n : 3 * n] + power[:, 3 * n :]
    measured = amplitudes[k]
    residual = (intensity - measured * measured) * scale
    weighted = far * jnp.concatenate([jnp.concatenate([residual] * MODES, 1)] * 2, 0)
    back = right_dft(to_rows(left_dft(li[...], weighted)), ri[...])
    total_r = total_i = None
    for m in range(MODES):
        gr, gi = back[m * n : (m + 1) * n, :n], back[m * n : (m + 1) * n, n:]
        pr, pi = probe[m, 0], probe[m, 1]
        tr, ti = pr * gr + pi * gi, pr * gi - pi * gr
        total_r, total_i = (tr, ti) if m == 0 else (total_r + tr, total_i + ti)
        probe_total[m, 0] += obj_r * gr + obj_i * gi
        probe_total[m, 1] += obj_r * gi - obj_i * gr
    patch_grads[out_slot, 0] = total_r
    patch_grads[out_slot, 1] = total_i


def run_slots(counts, offsets, chosen, early, *work):
    size = choose_slots(counts, offsets, chosen, early)

    def step(j, carry):
        for u in range(UNROLL):
            i = j * UNROLL + u
            on = i < size
            k = jnp.where(on, chosen[jnp.minimum(i, SLOTS - 1)], 0)
            slot_work(k, jnp.where(on, k, SLOTS), jnp.where(on, 2.0, 0.0), offsets, *work)
        return carry

    lax.fori_loop(0, (size + UNROLL - 1) // UNROLL, step, 0)


def tile_copies(tile, extended, sem):
    return [
        pltpu.make_async_copy(
            tile.at[:, :, pl.ds(b * PATCH, PATCH)], extended.at[:, b + 1, pl.ds(HALF, TILE), :], sem
        )
        for b in range(TILE // PATCH)
    ]


def early_kernel(counts, offsets, tile, amps, probe, rf, lf, li, ri, patch_grads, probe_total, extended, chosen, sem):
    copies = tile_copies(tile, extended, sem)
    for c in copies:
        c.start()
    probe_total[...] = jnp.zeros_like(probe_total)
    for c in copies:
        c.wait()
    run_slots(counts, offsets, chosen, True, extended, amps, probe, (rf, lf, li, ri), patch_grads, probe_total)


def late_kernel(
    counts, offsets, tile, above, below, left, right, amps, probe, rf, lf, li, ri, probe_before,
    patch_grads, probe_total, extended, chosen, sem
):
    copies = tile_copies(tile, extended, sem)
    for b in range(TILE // PATCH):
        lanes = pl.ds(b * PATCH, PATCH)
        copies.append(pltpu.make_async_copy(above.at[:, :, lanes], extended.at[:, b + 1, pl.ds(0, HALF), :], sem))
        copies.append(
            pltpu.make_async_copy(below.at[:, :, lanes], extended.at[:, b + 1, pl.ds(HALF + TILE, HALF), :], sem)
        )
    for c in copies:
        c.start()
    probe_total[...] = probe_before[...]
    extended[0, 0] = pltpu.roll(left[...], HALF, 1)
    extended[1, 0] = left[...]
    extended[0, BLOCKS - 1] = right[...]
    extended[1, BLOCKS - 1] = pltpu.roll(right[...], HALF, 1)
    for c in copies:
        c.wait()
    run_slots(counts, offsets, chosen, False, extended, amps, probe, (rf, lf, li, ri), patch_grads, probe_total)


def pack_kernel(above, below, first, last, left_send, right_send):
    def pack(rows, a, b):
        low = lane_iota(rows) < HALF
        left_send_part = jnp.where(low, a[0], pltpu.roll(a[1], HALF, 1))
        right_send_part = jnp.where(low, pltpu.roll(b[0], HALF, 1), b[1])
        return left_send_part, right_send_part

    end = TILE - PATCH
    for start, rows, a, b in (
        (0, HALF, above[:, :, :PATCH], above[:, :, end:]),
        (HALF, TILE, first[...], last[...]),
        (HALF + TILE, HALF, below[:, :, :PATCH], below[:, :, end:]),
    ):
        left_send[start : start + rows, :], right_send[start : start + rows, :] = pack(rows, a, b)


def deposit_kernel(counts, offsets, early_grads, late_grads, middle, left_send, right_send, total, held, sems):
    n = PATCH
    live, first = early_slots(counts, offsets)

    def fetch(k, seen, buffer):
        is_early = is_inside(offsets, k) & (seen < first)

        @pl.when(is_early)
        def _():
            pltpu.make_async_copy(early_grads.at[k], held.at[k], sems.at[k]).start()

        @pl.when(jnp.logical_not(is_early))
        def _():
            pltpu.make_async_copy(late_grads.at[k], held.at[k], sems.at[k]).start()

        return seen + jnp.where(is_inside(offsets, k), 1, 0)

    lax.fori_loop(0, live, lambda k, seen: fetch(k, seen, 0), 0)
    total[...] = jnp.zeros_like(total)
    lane = lane_iota(n)

    def add(k, carry):
        pltpu.make_async_copy(early_grads.at[k], held.at[k], sems.at[k]).wait()
        row = offsets[2 * k] + HALF
        col = offsets[2 * k + 1] + n
        block = col // n
        lead = col - block * n
        for p in range(2):
            turned = pltpu.roll(held[k, p], lead, 1)
            total[p, block, pl.ds(row, n), :] += jnp.where(lane >= lead, turned, 0.0)
            total[p, block + 1, pl.ds(row, n), :] += jnp.where(lane < lead, turned, 0.0)
        return carry

    lax.fori_loop(0, live, add, 0)
    for b in range(TILE // n):
        middle[:, :, b * n : (b + 1) * n] = total[:, b + 1]
    low = lane_iota(EXT) < HALF
    left_send[...] = jnp.where(low, pltpu.roll(total[0, 0], HALF, 1), total[1, 0])
    right_send[...] = jnp.where(low, total[0, BLOCKS - 1], pltpu.roll(total[1, BLOCKS - 1], HALF, 1))


def add_sides(rows, middle, from_left, from_right):
    low = lane_iota(rows) < HALF
    first = [
        middle[0, :, :PATCH] + jnp.where(low, from_left, 0.0),
        middle[1, :, :PATCH] + jnp.where(low, pltpu.roll(from_left, HALF, 1), 0.0),
    ]
    end = TILE - PATCH
    last = [
        middle[0, :, end:] + jnp.where(low, 0.0, pltpu.roll(from_right, HALF, 1)),
        middle[1, :, end:] + jnp.where(low, 0.0, from_right),
    ]
    return [jnp.concatenate([first[p], middle[p, :, PATCH:end], last[p]], 1) for p in range(2)]


def edges_kernel(middle_top, middle_bottom, from_left, from_right, top_send, bottom_send):
    for part, rows, out in (
        (middle_top, slice(0, HALF), top_send),
        (middle_bottom, slice(HALF + TILE, EXT), bottom_send),
    ):
        out[0], out[1] = add_sides(HALF, part[...], from_left[rows, :], from_right[rows, :])


def merge_kernel(middle, from_left, from_right, from_above, from_below, out):
    rows = slice(HALF, HALF + TILE)
    whole = add_sides(TILE, middle[:, rows, :], from_left[rows, :], from_right[rows, :])
    for p in range(2):
        out[p, HALF : TILE - HALF, :] = whole[p][HALF : TILE - HALF]
        out[p, :HALF, :] = whole[p][:HALF] + from_above[p]
        out[p, TILE - HALF :, :] = whole[p][TILE - HALF :] + from_below[p]


VMEM = pl.BlockSpec(memory_space=pltpu.VMEM)
SMEM = pl.BlockSpec(memory_space=pltpu.SMEM)
ANY = pl.BlockSpec(memory_space=pl.ANY)


def call(kernel, in_specs, out_shapes, scratch, *args, out_specs=None):
    return pl.pallas_call(
        kernel,
        in_specs=in_specs,
        out_specs=out_specs or [VMEM] * len(out_shapes),
        out_shape=[jax.ShapeDtypeStruct(s, jnp.float32) for s in out_shapes],
        scratch_shapes=scratch,
        compiler_params=pltpu.CompilerParams(vmem_limit_bytes=48 * 2**20),
    )(*args)


def shift(value, axes, count, step):
    pairs = [(i, i + step) for i in range(count) if 0 <= i + step < count]
    return lax.ppermute(value, axes, pairs)


def swap(value, axis, bit, size):
    return lax.ppermute(value, axis, [(i, i ^ (1 << bit)) for i in range(size)])


def all_sum(x, sizes):
    halved = [("core", 0), ("zl", 0), ("y", 0), ("y", 1)]
    doubled = [("x", 0), ("x", 1), ("zh", 0), ("zh", 1)]
    for axis, bit in halved:
        half = x.shape[0] // 2
        mine = (lax.axis_index(axis) >> bit) & 1
        kept = lax.dynamic_slice_in_dim(x, mine * half, half, 0)
        sent = lax.dynamic_slice_in_dim(x, (1 - mine) * half, half, 0)
        x = kept + swap(sent, axis, bit, sizes[axis])
    for axis, bit in doubled:
        x = x + swap(x, axis, bit, sizes[axis])
    for axis, bit in reversed(halved):
        mine = (lax.axis_index(axis) >> bit) & 1
        other = swap(x, axis, bit, sizes[axis])
        x = jnp.where(mine == 0, jnp.concatenate([x, other], 0), jnp.concatenate([other, x], 0))
    return x


def per_device(sizes, tile, probe, amplitudes, offsets, counts):
    rows, cols = sizes["zh"] * sizes["x"], sizes["y"] * sizes["zl"] * sizes["core"]
    tables = [jnp.asarray(t) for t in dft_tables(PATCH)]
    counts = counts.reshape(1)
    offsets = offsets.reshape(2 * SLOTS)
    amps = amplitudes.reshape(SLOTS, PATCH, PATCH)
    from_above = shift(tile[:, TILE - HALF :, :], ROW, rows, 1)
    from_below = shift(tile[:, :HALF, :], ROW, rows, -1)
    slot_scratch = [
        pltpu.VMEM((2, BLOCKS, EXT, PATCH), jnp.float32),
        pltpu.SMEM((SLOTS + 1,), jnp.int32),
        pltpu.SemaphoreType.DMA,
    ]
    slot_shapes = [(SLOTS + 1, 2, PATCH, PATCH), (MODES, 2, PATCH, PATCH)]
    early_grads, probe_early = call(
        early_kernel, [SMEM, SMEM, ANY] + [VMEM] * 6, slot_shapes, slot_scratch, counts, offsets, tile, amps, probe, *tables
    )
    left_send, right_send = call(
        pack_kernel, [VMEM] * 4, [(EXT, PATCH)] * 2, [], from_above, from_below, tile[:, :, :PATCH], tile[:, :, TILE - PATCH :]
    )
    from_left = shift(right_send, COL, cols, 1)
    from_right = shift(left_send, COL, cols, -1)
    late_grads, probe_total = call(
        late_kernel, [SMEM, SMEM] + [ANY] * 3 + [VMEM] * 9, slot_shapes, slot_scratch,
        counts, offsets, tile, from_above, from_below, from_left, from_right, amps, probe, *tables, probe_early
    )
    factor = 1.0 / math.sqrt(rows * cols * SLOTS)
    summed = all_sum(probe_total.reshape(-1, PATCH), sizes)
    probe_grad = (summed * factor).reshape(MODES, 2, PATCH, PATCH)
    middle, left_out, right_out = call(
        deposit_kernel, [SMEM, SMEM, ANY, ANY], [(2, EXT, TILE), (EXT, PATCH), (EXT, PATCH)],
        [
            pltpu.VMEM((2, BLOCKS, EXT, PATCH), jnp.float32),
            pltpu.VMEM((SLOTS, 2, PATCH, PATCH), jnp.float32),
            pltpu.SemaphoreType.DMA((SLOTS,)),
        ],
        counts, offsets, early_grads, late_grads
    )
    grad_left = shift(right_out, COL, cols, 1)
    grad_right = shift(left_out, COL, cols, -1)
    top_out, bottom_out = call(
        edges_kernel, [VMEM] * 4, [(2, HALF, TILE)] * 2, [],
        middle[:, :HALF, :], middle[:, HALF + TILE :, :], grad_left, grad_right
    )
    grad_above = shift(bottom_out, ROW, rows, 1)
    grad_below = shift(top_out, ROW, rows, -1)
    (object_grad,) = call(
        merge_kernel, [VMEM] * 5, [(2, TILE, TILE)], [], middle, grad_left, grad_right, grad_above, grad_below
    )
    return object_grad, probe_grad


def solution(mesh):
    sizes = {"zh": 4, "x": 4, "y": 4, "zl": 2, "core": 2}
    fine = Mesh(mesh.devices.reshape(tuple(sizes.values())), tuple(sizes))
    return jax.shard_map(
        functools.partial(per_device, sizes),
        mesh=fine,
        in_specs=(P(None, ROW, COL), P(), P(ROW, COL), P(ROW, COL), P(ROW, COL)),
        out_specs=(P(None, ROW, COL), P()),
        check_vma=False,
    )
```

```python
import functools
import math

import jax
import jax.numpy as jnp
import ml_dtypes
import numpy as np
from jax import lax
from jax.experimental import pallas as pl
from jax.experimental.pallas import tpu as pltpu
from jax.sharding import Mesh
from jax.sharding import PartitionSpec as P

PATCH = 128
MODES = 4
TILE = 512
SLOTS = 16
HALF = 64
EXT = TILE + 2 * HALF
BLOCKS = 6
GROUP = 4

ROW = ("zh", "x")
COL = ("y", "zl", "core")


def split_table(table):
    high = table.astype(np.float32).astype(ml_dtypes.bfloat16)
    low = (table - high.astype(np.float64)).astype(np.float32).astype(ml_dtypes.bfloat16)
    return high, low


def dft_tables(n):
    i = np.arange(n)
    angles = (np.outer(i, i) % n) * (2 * math.pi / n)
    cos, sin = np.cos(angles) / math.sqrt(n), -np.sin(angles) / math.sqrt(n)
    forward = np.block([[cos, sin], [-sin, cos]])
    fh, fl = split_table(forward)
    ih, il = split_table(forward.T)
    return np.stack([fh, fl]), np.stack([ih, il])


def split(x):
    high = x.astype(jnp.bfloat16)
    return high, (x - high.astype(jnp.float32)).astype(jnp.bfloat16)


def dot(a, b):
    return jnp.dot(a, b, preferred_element_type=jnp.float32)


def right_dft(x, table):
    high, low = split(x)
    return dot(high, table[0]) + dot(low, table[0]) + dot(high, table[1])


def left_dft(table, x):
    high, low = split(x)
    return dot(table[0], high) + dot(table[1], high) + dot(table[0], low)


def to_cols(y):
    n = PATCH
    return jnp.concatenate(
        [jnp.concatenate([y[m * n : (m + 1) * n, p * n : (p + 1) * n] for m in range(MODES)], 1) for p in range(2)], 0
    )


def to_rows(z):
    n = PATCH
    return jnp.concatenate(
        [jnp.concatenate([z[p * n : (p + 1) * n, m * n : (m + 1) * n] for p in range(2)], 1) for m in range(MODES)], 0
    )


def lane_iota(rows):
    return lax.broadcasted_iota(jnp.int32, (rows, PATCH), 1)


def is_inside(offsets, k):
    r, c = offsets[0, 0, 0, k], offsets[0, 0, 1, k]
    top = TILE - PATCH
    return (r >= 0) & (r <= top) & (c >= 0) & (c <= top)


def early_slots(counts, offsets):
    live = counts[0, 0]

    def tally(k, total):
        return total + jnp.where(is_inside(offsets, k) & (k < live), 1, 0)

    inside = lax.fori_loop(0, SLOTS, tally, 0)
    return live, inside // 2 * 2


def choose_slots(counts, offsets, chosen, early):
    live, first = early_slots(counts, offsets)

    def pick(k, state):
        seen, size = state
        inner = is_inside(offsets, k)
        is_early = inner & (seen < first)
        chosen[size] = k
        take = (is_early == early) & (k < live)
        seen = seen + jnp.where(inner, 1, 0)
        return seen, size + jnp.where(take, 1, 0)

    _, size = lax.fori_loop(0, SLOTS, pick, (0, 0))
    return size


def slot_work(k, out_slot, scale, offsets, extended, amplitudes, probe, tables, patch_grads, probe_total):
    forward, inverse = tables
    n = PATCH
    row = offsets[0, 0, 0, k] + HALF
    col = offsets[0, 0, 1, k] + PATCH
    block = col // n
    lead = col - block * n
    turn = jnp.where(lead == 0, 0, n - lead)
    lane = lane_iota(n)
    parts = []
    for p in range(2):
        a = pltpu.roll(extended[p, block, pl.ds(row, n), :], turn, 1)
        b = pltpu.roll(extended[p, block + 1, pl.ds(row, n), :], turn, 1)
        parts.append(jnp.where(lane < n - lead, a, b))
    obj_r, obj_i = parts
    waves = []
    for m in range(MODES):
        pr, pi = probe[m, 0], probe[m, 1]
        waves.append(jnp.concatenate([pr * obj_r - pi * obj_i, pr * obj_i + pi * obj_r], 1))
    far = left_dft(inverse, to_cols(right_dft(jnp.concatenate(waves, 0), forward)))
    power = far * far
    power = power[:n] + power[n:]
    intensity = power[:, :n] + power[:, n : 2 * n] + power[:, 2 * n : 3 * n] + power[:, 3 * n :]
    measured = amplitudes[k]
    residual = (intensity - measured * measured) * scale
    weighted = far * jnp.concatenate([jnp.concatenate([residual] * MODES, 1)] * 2, 0)
    back = right_dft(to_rows(left_dft(forward, weighted)), inverse)
    total_r = total_i = None
    for m in range(MODES):
        gr, gi = back[m * n : (m + 1) * n, :n], back[m * n : (m + 1) * n, n:]
        pr, pi = probe[m, 0], probe[m, 1]
        tr, ti = pr * gr + pi * gi, pr * gi - pi * gr
        total_r, total_i = (tr, ti) if m == 0 else (total_r + tr, total_i + ti)
        probe_total[m, 0] += obj_r * gr + obj_i * gi
        probe_total[m, 1] += obj_r * gi - obj_i * gr
    patch_grads[out_slot, 0] = total_r
    patch_grads[out_slot, 1] = total_i


def tile_copies(tile, extended, sem):
    return [
        pltpu.make_async_copy(
            tile.at[:, :, pl.ds(b * PATCH, PATCH)], extended.at[:, b + 1, pl.ds(HALF, TILE), :], sem
        )
        for b in range(TILE // PATCH)
    ]


def run_slots(early, counts, offsets, amps, patch_grads, probe_in, probe_total, scratch, copies, others=()):
    extended, measured, probe, grads, forward, inverse, chosen, sem, out_sems = scratch
    copies = copies + [pltpu.make_async_copy(amps, measured, sem), pltpu.make_async_copy(probe_in, probe, sem)]
    for c in copies:
        c.start()
    size = choose_slots(counts, offsets, chosen, early)
    for c in [*copies, *others]:
        c.wait()

    def step(first, count):
        for u in range(count):
            i = first + u
            on = i < size
            k = jnp.where(on, chosen[jnp.minimum(i, SLOTS - 1)], 0)
            out = jnp.where(on, k, SLOTS)
            scale = jnp.where(on, 2.0, 0.0)
            slot_work(k, out, scale, offsets, extended, measured, probe, (forward, inverse), grads, probe_total)
        for u in range(count):
            i = first + u

            @pl.when(i < size)
            def _():
                k = chosen[i]
                pltpu.make_async_copy(grads.at[k], patch_grads.at[k], out_sems.at[k]).start()

    whole = size // GROUP * GROUP

    def group(j, carry):
        step(j * GROUP, GROUP)
        return carry

    def pair(j, carry):
        step(whole + j * 2, 2)
        return carry

    lax.fori_loop(0, size // GROUP, group, 0)
    lax.fori_loop(0, (size - whole + 1) // 2, pair, 0)

    def finish(i, carry):
        k = chosen[i]
        pltpu.make_async_copy(grads.at[k], patch_grads.at[k], out_sems.at[k]).wait()
        return carry

    lax.fori_loop(0, size, finish, 0)


def early_kernel(counts, offsets, tile, amps, probe, forward, inverse, patch_grads, probe_total, *scratch):
    extended, sem = scratch[0], scratch[-2]
    copies = tile_copies(tile, extended, sem) + [
        pltpu.make_async_copy(forward, scratch[4], sem),
        pltpu.make_async_copy(inverse, scratch[5], sem),
    ]
    probe_total[...] = jnp.zeros_like(probe_total)
    run_slots(True, counts, offsets, amps, patch_grads, probe, probe_total, scratch, copies)


def late_kernel(
    counts, offsets, sides, tile, rows_a, rows_b, amps, probe, forward, inverse, cols_a, cols_b, corners_a, corners_b,
    probe_before, patch_grads, probe_total, *scratch
):
    extended, side_sem, sem = scratch[0], scratch[-3], scratch[-2]
    scratch = scratch[:-3] + scratch[-2:]
    copies = tile_copies(tile, extended, sem) + [
        pltpu.make_async_copy(forward, scratch[4], sem),
        pltpu.make_async_copy(inverse, scratch[5], sem),
    ]
    even_row, even_col = sides[0] == 0, sides[1] == 0

    def strip_copies(above, below):
        return [
            pltpu.make_async_copy(
                source.at[:, :, pl.ds(b * PATCH, PATCH)], extended.at[:, b + 1, pl.ds(top, HALF), :], side_sem
            )
            for source, top in ((above, 0), (below, HALF + TILE))
            for b in range(TILE // PATCH)
        ]

    def start(above, below):
        for c in strip_copies(above, below):
            c.start()

    @pl.when(even_row)
    def _():
        start(rows_b, rows_a)

    @pl.when(jnp.logical_not(even_row))
    def _():
        start(rows_a, rows_b)

    probe_total[...] = probe_before[...]

    def columns(left, right, left_corners, right_corners):
        for rows, l, r in (
            (pl.ds(HALF, TILE), left[...], right[...]),
            (pl.ds(0, HALF), left_corners[:HALF, :], right_corners[:HALF, :]),
            (pl.ds(HALF + TILE, HALF), left_corners[HALF:, :], right_corners[HALF:, :]),
        ):
            extended[0, 0, rows, :] = pltpu.roll(l, HALF, 1)
            extended[1, 0, rows, :] = l
            extended[0, BLOCKS - 1, rows, :] = r
            extended[1, BLOCKS - 1, rows, :] = pltpu.roll(r, HALF, 1)

    @pl.when(even_col)
    def _():
        columns(cols_b, cols_a, corners_b, corners_a)

    @pl.when(jnp.logical_not(even_col))
    def _():
        columns(cols_a, cols_b, corners_a, corners_b)

    run_slots(
        False, counts, offsets, amps, patch_grads, probe, probe_total, scratch, copies, strip_copies(rows_a, rows_b)
    )


def put_by_side(even, a, b, after, before):
    @pl.when(even)
    def _():
        a[...] = after
        b[...] = before

    @pl.when(jnp.logical_not(even))
    def _():
        a[...] = before
        b[...] = after


def pack_kernel(sides, tile, cols_a, cols_b, first, last, sem):
    copies = [
        pltpu.make_async_copy(tile.at[:, :, pl.ds(0, PATCH)], first, sem),
        pltpu.make_async_copy(tile.at[:, :, pl.ds(TILE - PATCH, PATCH)], last, sem),
    ]
    for c in copies:
        c.start()
    for c in copies:
        c.wait()
    low = lane_iota(TILE) < HALF
    put_by_side(
        sides[1] == 0,
        cols_a,
        cols_b,
        jnp.where(low, pltpu.roll(last[0], HALF, 1), last[1]),
        jnp.where(low, first[0], pltpu.roll(first[1], HALF, 1)),
    )


def pack_corners_kernel(sides, rows_a, rows_b, corners_a, corners_b, first, last, sem):
    even_row = sides[0] == 0
    copies = []
    for i, source in enumerate((rows_a, rows_b)):
        copies.append(pltpu.make_async_copy(source.at[:, :, pl.ds(0, PATCH)], first.at[i], sem))
        copies.append(pltpu.make_async_copy(source.at[:, :, pl.ds(TILE - PATCH, PATCH)], last.at[i], sem))
    for c in copies:
        c.start()
    for c in copies:
        c.wait()
    low = lane_iota(HALF) < HALF
    for i in range(2):
        l = jnp.where(even_row, first[1 - i], first[i])
        r = jnp.where(even_row, last[1 - i], last[i])
        rows = pl.ds(i * HALF, HALF)
        put_by_side(
            sides[1] == 0,
            corners_a.at[rows, :],
            corners_b.at[rows, :],
            jnp.where(low, pltpu.roll(r[0], HALF, 1), r[1]),
            jnp.where(low, l[0], pltpu.roll(l[1], HALF, 1)),
        )


def deposit_kernel(
    counts, offsets, sides, early_grads, late_grads, inner, rows_a, rows_b, cols_a, cols_b, total, held, flank, sems, out_sem
):
    n = PATCH
    live, first = early_slots(counts, offsets)

    def fetch(k, seen):
        inside = is_inside(offsets, k)
        is_early = inside & (seen < first)

        @pl.when(is_early)
        def _():
            pltpu.make_async_copy(early_grads.at[k], held.at[k], sems.at[k]).start()

        @pl.when(jnp.logical_not(is_early))
        def _():
            pltpu.make_async_copy(late_grads.at[k], held.at[k], sems.at[k]).start()

        return seen + jnp.where(inside, 1, 0)

    lax.fori_loop(0, live, fetch, 0)
    total[...] = jnp.zeros_like(total)
    lane = lane_iota(n)

    def turned(k):
        lead = (offsets[0, 0, 1, k] + n) % n
        pltpu.make_async_copy(early_grads.at[k], held.at[k], sems.at[k]).wait()
        return [pltpu.roll(held[k, p], lead, 1) for p in range(2)]

    def add(k, parts):
        row = offsets[0, 0, 0, k] + HALF
        col = offsets[0, 0, 1, k] + n
        block = col // n
        lead = col - block * n
        rows = pl.ds(row, n)
        old = [[total[p, block + i, rows, :] for i in range(2)] for p in range(2)]
        for p in range(2):
            total[p, block, rows, :] = old[p][0] + jnp.where(lane >= lead, parts[p], 0.0)
            total[p, block + 1, rows, :] = old[p][1] + jnp.where(lane < lead, parts[p], 0.0)

    def add_two(j, carry):
        one, two = turned(2 * j), turned(2 * j + 1)
        add(2 * j, one)
        add(2 * j + 1, two)
        return carry

    lax.fori_loop(0, live // 2, add_two, 0)

    @pl.when(live % 2 == 1)
    def _():
        add(live - 1, turned(live - 1))

    low = lane_iota(EXT) < HALF
    for p in range(2):
        flank[p] = pltpu.roll(jnp.where(low, total[p, BLOCKS - 1], total[p, 0]), HALF, 1)

    def copies(above, below):
        made = []
        for start, rows, out in ((0, HALF, above), (HALF, TILE, inner), (HALF + TILE, HALF, below)):
            for b in range(TILE // n):
                made.append((total.at[:, b + 1, pl.ds(start, rows), :], out.at[:, :, pl.ds(b * n, n)]))
        made.append((flank.at[:, pl.ds(0, HALF), :], above.at[:, :, pl.ds(TILE, n)]))
        made.append((flank.at[:, pl.ds(HALF + TILE, HALF), :], below.at[:, :, pl.ds(TILE, n)]))
        return [pltpu.make_async_copy(near, far, out_sem) for near, far in made]

    def start(above, below):
        for c in copies(above, below):
            c.start()

    @pl.when(sides[0] == 0)
    def _():
        start(rows_b, rows_a)

    @pl.when(sides[0] != 0)
    def _():
        start(rows_a, rows_b)

    low = lane_iota(TILE) < HALF
    own = flank[0, HALF : HALF + TILE, :], flank[1, HALF : HALF + TILE, :]
    put_by_side(
        sides[1] == 0,
        cols_a,
        cols_b,
        jnp.where(low, pltpu.roll(own[0], HALF, 1), own[1]),
        jnp.where(low, own[0], pltpu.roll(own[1], HALF, 1)),
    )
    for c in copies(rows_a, rows_b):
        c.wait()


def corner_kernel(sides, rows_a, rows_b, corners_a, corners_b, held, sem):
    even_row = sides[0] == 0
    copies = [pltpu.make_async_copy(r.at[:, :, pl.ds(TILE, PATCH)], held.at[i], sem) for i, r in enumerate((rows_a, rows_b))]
    for c in copies:
        c.start()
    for c in copies:
        c.wait()
    low = lane_iota(HALF) < HALF
    a, b = held[0], held[1]
    for i, part in enumerate((jnp.where(even_row, b, a), jnp.where(even_row, a, b))):
        rows = pl.ds(i * HALF, HALF)
        put_by_side(
            sides[1] == 0,
            corners_a.at[rows, :],
            corners_b.at[rows, :],
            jnp.where(low, pltpu.roll(part[0], HALF, 1), part[1]),
            jnp.where(low, part[0], pltpu.roll(part[1], HALF, 1)),
        )


def merge_kernel(
    sides, inner, rows_a, rows_b, cols_a, cols_b, corners_a, corners_b, out, left, right, top, bottom, strips, sems, sem
):
    end = TILE - PATCH
    regions = (
        (out.at[:, :, pl.ds(0, PATCH)], left),
        (out.at[:, :, pl.ds(end, PATCH)], right),
        (out.at[:, pl.ds(0, HALF), pl.ds(PATCH, TILE - 2 * PATCH)], top),
        (out.at[:, pl.ds(TILE - HALF, HALF), pl.ds(PATCH, TILE - 2 * PATCH)], bottom),
    )
    loads = [pltpu.make_async_copy(far, near, sems.at[i]) for i, (far, near) in enumerate(regions)]
    loads += [pltpu.make_async_copy(r.at[:, :, pl.ds(0, TILE)], strips.at[i], sem) for i, r in enumerate((rows_a, rows_b))]
    for c in loads:
        c.start()
    even_row, even_col = sides[0] == 0, sides[1] == 0

    def both_sides(a, b):
        low = lane_iota(a.shape[0]) < HALF
        from_left, from_right = jnp.where(even_col, b, a), jnp.where(even_col, a, b)
        first = (jnp.where(low, from_left, 0.0), jnp.where(low, pltpu.roll(from_left, HALF, 1), 0.0))
        last = (jnp.where(low, 0.0, pltpu.roll(from_right, HALF, 1)), jnp.where(low, 0.0, from_right))
        return first, last

    sides_terms = both_sides(cols_a[...], cols_b[...])
    corner_terms = both_sides(corners_a[...], corners_b[...])
    for c in loads:
        c.wait()
    a, b = strips[0], strips[1]
    above, below = jnp.where(even_row, b, a), jnp.where(even_row, a, b)
    middle = slice(PATCH, end)
    for p in range(2):
        for i, (near, lanes) in enumerate(((left, slice(0, PATCH)), (right, slice(end, TILE)))):
            near[p] += sides_terms[i][p]
            near[p, :HALF, :] += above[p, :, lanes] + corner_terms[i][p][:HALF]
            near[p, TILE - HALF :, :] += below[p, :, lanes] + corner_terms[i][p][HALF:]
        top[p] += above[p, :, middle]
        bottom[p] += below[p, :, middle]
    stores = [pltpu.make_async_copy(near, far, sems.at[i]) for i, (far, near) in enumerate(regions)]
    for c in stores:
        c.start()
    for c in stores:
        c.wait()


VMEM = pl.BlockSpec(memory_space=pltpu.VMEM)
SMEM = pl.BlockSpec(memory_space=pltpu.SMEM)
HBM = pl.BlockSpec(memory_space=pltpu.HBM)


def call(kernel, in_specs, out_specs, out_shapes, scratch, *args, aliases=None, limit=62):
    return pl.pallas_call(
        kernel,
        in_specs=in_specs,
        out_specs=out_specs,
        out_shape=[jax.ShapeDtypeStruct(s, jnp.float32) for s in out_shapes],
        scratch_shapes=scratch,
        input_output_aliases=aliases or {},
        compiler_params=pltpu.CompilerParams(vmem_limit_bytes=limit * 2**20),
    )(*args)


def swap(value, axes, size, first):
    pairs = [(i, i + 1) for i in range(first, size - 1, 2)]
    return lax.ppermute(value, axes, pairs + [(j, i) for i, j in pairs])


def halve(x, axis):
    half, me = x.shape[0] // 2, lax.axis_index(axis)
    sent = lax.dynamic_slice_in_dim(x, (1 - me) * half, half, 0)
    return lax.dynamic_slice_in_dim(x, me * half, half, 0) + swap(sent, axis, 2, 0)


def double(x, axis):
    other, me = swap(x, axis, 2, 0), lax.axis_index(axis)
    return jnp.where(me == 0, jnp.concatenate([x, other], 0), jnp.concatenate([other, x], 0))


def deal(x, axes, sizes):
    count = math.prod(sizes[a] for a in axes)
    return lax.all_to_all(x.reshape(count, -1, PATCH), axes, 0, 0, tiled=True)


def spread(x, axes, sizes):
    count = math.prod(sizes[a] for a in axes)
    return lax.all_to_all(jnp.broadcast_to(x[None], (count, *x.shape)), axes, 0, 0, tiled=True)


def per_device(sizes, tile, probe, amplitudes, offsets, counts):
    rows, cols = sizes["zh"] * sizes["x"], sizes["y"] * sizes["zl"] * sizes["core"]
    forward, inverse = [jnp.asarray(t) for t in dft_tables(PATCH)]
    offsets = offsets.transpose(0, 1, 3, 2)
    amps = amplitudes.reshape(SLOTS, PATCH, PATCH)
    odd_row, odd_col = lax.axis_index(ROW) % 2, lax.axis_index(COL) % 2
    sides = jnp.stack([odd_row, odd_col]).astype(jnp.int32)
    wide = 2 * PATCH
    slot_scratch = [
        pltpu.VMEM((2, BLOCKS, EXT, PATCH), jnp.float32),
        pltpu.VMEM((SLOTS, PATCH, PATCH), jnp.float32),
        pltpu.VMEM((MODES, 2, PATCH, PATCH), jnp.float32),
        pltpu.VMEM((SLOTS + 1, 2, PATCH, PATCH), jnp.float32),
        pltpu.VMEM((2, wide, wide), jnp.bfloat16),
        pltpu.VMEM((2, wide, wide), jnp.bfloat16),
        pltpu.SMEM((SLOTS + 1,), jnp.int32),
        pltpu.SemaphoreType.DMA,
        pltpu.SemaphoreType.DMA((SLOTS,)),
    ]
    grads_shape, probe_shape = (SLOTS, 2, PATCH, PATCH), (MODES, 2, PATCH, PATCH)
    wide_row, column = (2, HALF, TILE + PATCH), (TILE, PATCH)
    block = pltpu.VMEM((2, TILE, PATCH), jnp.float32)
    low, high = 0, TILE - HALF
    after = lax.dynamic_slice_in_dim(tile, jnp.where(odd_row == 0, high, low), HALF, 1)
    before = lax.dynamic_slice_in_dim(tile, jnp.where(odd_row == 0, low, high), HALF, 1)
    rows_b = swap(before, ROW, rows, 1)
    rows_a = swap(after, ROW, rows, 0)
    cols_a, cols_b = call(
        pack_kernel, [SMEM, HBM], [VMEM] * 2, [column] * 2, [block, block, pltpu.SemaphoreType.DMA], sides, tile, limit=16
    )
    cols_b = swap(cols_b, COL, cols, 1)
    cols_a = swap(cols_a, COL, cols, 0)
    early_grads, probe_early = call(
        early_kernel, [SMEM] * 2 + [HBM] * 5, [HBM, VMEM], [grads_shape, probe_shape], slot_scratch,
        counts, offsets, tile, amps, probe, forward, inverse
    )
    rows_a, rows_b, probe_early = lax.optimization_barrier((rows_a, rows_b, probe_early))
    piece = pltpu.VMEM((2, 2, HALF, PATCH), jnp.float32)
    corners_a, corners_b = call(
        pack_corners_kernel, [SMEM] + [HBM] * 2, [VMEM] * 2, [(PATCH, PATCH)] * 2, [piece, piece, pltpu.SemaphoreType.DMA],
        sides, rows_a, rows_b, limit=16
    )
    corners_b = swap(corners_b, COL, cols, 1)
    corners_a = swap(corners_a, COL, cols, 0)
    late_scratch = slot_scratch[:-2] + [pltpu.SemaphoreType.DMA] + slot_scratch[-2:]
    late_grads, probe_total = call(
        late_kernel, [SMEM] * 3 + [HBM] * 7 + [VMEM] * 5, [HBM, VMEM], [grads_shape, probe_shape], late_scratch,
        counts, offsets, sides, tile, rows_a, rows_b, amps, probe, forward, inverse, cols_a, cols_b, corners_a, corners_b, probe_early
    )

    sums = halve(probe_total.reshape(-1, PATCH), "core")
    inner, rows_a, rows_b, cols_a, cols_b = call(
        deposit_kernel, [SMEM] * 3 + [HBM] * 2, [HBM] * 3 + [VMEM] * 2,
        [(2, TILE, TILE), wide_row, wide_row, column, column],
        [
            pltpu.VMEM((2, BLOCKS, EXT, PATCH), jnp.float32),
            pltpu.VMEM(grads_shape, jnp.float32),
            pltpu.VMEM((2, EXT, PATCH), jnp.float32),
            pltpu.SemaphoreType.DMA((SLOTS,)),
            pltpu.SemaphoreType.DMA,
        ],
        counts, offsets, sides, early_grads, late_grads
    )
    rows_b = swap(rows_b, ROW, rows, 1)
    cols_b = swap(cols_b, COL, cols, 1)
    rows_a = swap(rows_a, ROW, rows, 0)
    cols_a = swap(cols_a, COL, cols, 0)
    plane, line = ("x", "y"), ("zh", "zl")
    sums = jnp.sum(deal(sums, plane, sizes), 0)
    sums = jnp.sum(spread(sums, line, sizes), 0)
    sums, rows_a, rows_b, cols_a, cols_b = lax.optimization_barrier((sums, rows_a, rows_b, cols_a, cols_b))
    corners_a, corners_b = call(
        corner_kernel, [SMEM] + [HBM] * 2, [VMEM] * 2, [(PATCH, PATCH)] * 2, [piece, pltpu.SemaphoreType.DMA],
        sides, rows_a, rows_b, limit=16
    )
    corners_b = swap(corners_b, COL, cols, 1)
    corners_a = swap(corners_a, COL, cols, 0)
    sums = spread(sums, plane, sizes).reshape(-1, PATCH)
    sums, corners_a, corners_b = lax.optimization_barrier((sums, corners_a, corners_b))
    end = pltpu.VMEM((2, HALF, TILE - 2 * PATCH), jnp.float32)
    (object_grad,) = call(
        merge_kernel, [SMEM] + [HBM] * 3 + [VMEM] * 4, [HBM], [(2, TILE, TILE)],
        [block, block, end, end, pltpu.VMEM((2, 2, HALF, TILE), jnp.float32), pltpu.SemaphoreType.DMA((4,)), pltpu.SemaphoreType.DMA],
        sides, inner, rows_a, rows_b, cols_a, cols_b, corners_a, corners_b, aliases={1: 0}, limit=16
    )
    factor = 1.0 / math.sqrt(rows * cols * SLOTS)
    probe_grad = (double(sums, "core") * factor).reshape(probe_shape)
    return object_grad, probe_grad


def solution(mesh):
    sizes = {"zh": 4, "x": 4, "y": 4, "zl": 2, "core": 2}
    fine = Mesh(mesh.devices.reshape(tuple(sizes.values())), tuple(sizes))
    return jax.shard_map(
        functools.partial(per_device, sizes),
        mesh=fine,
        in_specs=(P(None, ROW, COL), P(), P(ROW, COL), P(ROW, COL), P(ROW, COL)),
        out_specs=(P(None, ROW, COL), P()),
        check_vma=False,
    )
```

```python
import functools
import math

import jax
import jax.numpy as jnp
import ml_dtypes
import numpy as np
from jax import lax
from jax.experimental import pallas as pl
from jax.experimental.pallas import tpu as pltpu
from jax.sharding import Mesh
from jax.sharding import PartitionSpec as P

PATCH = 128
MODES = 4
TILE = 512
SLOTS = 16
HALF = 64
EXT = TILE + 2 * HALF
BLOCKS = 6
GROUP = 4

ROW = ("zh", "x")
COL = ("y", "zl", "core")


def split_table(table):
    high = table.astype(np.float32).astype(ml_dtypes.bfloat16)
    low = (table - high.astype(np.float64)).astype(np.float32).astype(ml_dtypes.bfloat16)
    return high, low


def dft_tables(n):
    i = np.arange(n)
    angles = (np.outer(i, i) % n) * (2 * math.pi / n)
    cos, sin = np.cos(angles) / math.sqrt(n), -np.sin(angles) / math.sqrt(n)
    forward = np.block([[cos, sin], [-sin, cos]])
    fh, fl = split_table(forward)
    ih, il = split_table(forward.T)
    return np.stack([fh, fl]), np.stack([ih, il])


def split(x):
    high = x.astype(jnp.bfloat16)
    return high, (x - high.astype(jnp.float32)).astype(jnp.bfloat16)


def dot(a, b):
    return jnp.dot(a, b, preferred_element_type=jnp.float32)


def right_dft(x, table):
    high, low = split(x)
    return dot(high, table[0]) + dot(low, table[0]) + dot(high, table[1])


def left_dft(table, x):
    high, low = split(x)
    return dot(table[0], high) + dot(table[1], high) + dot(table[0], low)


def to_cols(y):
    n = PATCH
    return jnp.concatenate(
        [jnp.concatenate([y[m * n : (m + 1) * n, p * n : (p + 1) * n] for m in range(MODES)], 1) for p in range(2)], 0
    )


def to_rows(z):
    n = PATCH
    return jnp.concatenate(
        [jnp.concatenate([z[p * n : (p + 1) * n, m * n : (m + 1) * n] for p in range(2)], 1) for m in range(MODES)], 0
    )


def lane_iota(rows):
    return lax.broadcasted_iota(jnp.int32, (rows, PATCH), 1)


def is_inside(offsets, k):
    r, c = offsets[0, 0, 0, k], offsets[0, 0, 1, k]
    top = TILE - PATCH
    return (r >= 0) & (r <= top) & (c >= 0) & (c <= top)


def early_slots(counts, offsets):
    live = counts[0, 0]

    def tally(k, total):
        return total + jnp.where(is_inside(offsets, k) & (k < live), 1, 0)

    inside = lax.fori_loop(0, SLOTS, tally, 0)
    return live, inside // 2 * 2


def choose_slots(counts, offsets, chosen, early):
    live, first = early_slots(counts, offsets)

    def pick(k, state):
        seen, size = state
        inner = is_inside(offsets, k)
        is_early = inner & (seen < first)
        chosen[size] = k
        take = (is_early == early) & (k < live)
        seen = seen + jnp.where(inner, 1, 0)
        return seen, size + jnp.where(take, 1, 0)

    _, size = lax.fori_loop(0, SLOTS, pick, (0, 0))
    return size


def slot_work(k, out_slot, scale, offsets, extended, amplitudes, probe, tables, patch_grads, probe_total):
    forward, inverse = tables
    n = PATCH
    row = offsets[0, 0, 0, k] + HALF
    col = offsets[0, 0, 1, k] + PATCH
    block = col // n
    lead = col - block * n
    turn = jnp.where(lead == 0, 0, n - lead)
    lane = lane_iota(n)
    parts = []
    for p in range(2):
        a = pltpu.roll(extended[p, block, pl.ds(row, n), :], turn, 1)
        b = pltpu.roll(extended[p, block + 1, pl.ds(row, n), :], turn, 1)
        parts.append(jnp.where(lane < n - lead, a, b))
    obj_r, obj_i = parts
    waves = []
    for m in range(MODES):
        pr, pi = probe[m, 0], probe[m, 1]
        waves.append(jnp.concatenate([pr * obj_r - pi * obj_i, pr * obj_i + pi * obj_r], 1))
    far = left_dft(inverse, to_cols(right_dft(jnp.concatenate(waves, 0), forward)))
    power = far * far
    power = power[:n] + power[n:]
    intensity = power[:, :n] + power[:, n : 2 * n] + power[:, 2 * n : 3 * n] + power[:, 3 * n :]
    measured = amplitudes[k]
    residual = (intensity - measured * measured) * scale
    weighted = far * jnp.concatenate([jnp.concatenate([residual] * MODES, 1)] * 2, 0)
    back = right_dft(to_rows(left_dft(forward, weighted)), inverse)
    total_r = total_i = None
    for m in range(MODES):
        gr, gi = back[m * n : (m + 1) * n, :n], back[m * n : (m + 1) * n, n:]
        pr, pi = probe[m, 0], probe[m, 1]
        tr, ti = pr * gr + pi * gi, pr * gi - pi * gr
        total_r, total_i = (tr, ti) if m == 0 else (total_r + tr, total_i + ti)
        probe_total[m, 0] += obj_r * gr + obj_i * gi
        probe_total[m, 1] += obj_r * gi - obj_i * gr
    patch_grads[out_slot, 0] = total_r
    patch_grads[out_slot, 1] = total_i


def tile_copies(tile, extended, sem):
    return [
        pltpu.make_async_copy(
            tile.at[:, :, pl.ds(b * PATCH, PATCH)], extended.at[:, b + 1, pl.ds(HALF, TILE), :], sem
        )
        for b in range(TILE // PATCH)
    ]


def run_slots(early, counts, offsets, amps, patch_grads, probe_in, probe_total, scratch, copies, others=()):
    extended, measured, probe, grads, forward, inverse, chosen, sem, out_sems = scratch
    copies = copies + [pltpu.make_async_copy(amps, measured, sem), pltpu.make_async_copy(probe_in, probe, sem)]
    for c in copies:
        c.start()
    size = choose_slots(counts, offsets, chosen, early)
    for c in [*copies, *others]:
        c.wait()

    def step(first, count):
        for u in range(count):
            i = first + u
            on = i < size
            k = jnp.where(on, chosen[jnp.minimum(i, SLOTS - 1)], 0)
            out = jnp.where(on, k, SLOTS)
            scale = jnp.where(on, 2.0, 0.0)
            slot_work(k, out, scale, offsets, extended, measured, probe, (forward, inverse), grads, probe_total)
        for u in range(count):
            i = first + u

            @pl.when(i < size)
            def _():
                k = chosen[i]
                pltpu.make_async_copy(grads.at[k], patch_grads.at[k], out_sems.at[k]).start()

    whole = size // GROUP * GROUP

    def group(j, carry):
        step(j * GROUP, GROUP)
        return carry

    def pair(j, carry):
        step(whole + j * 2, 2)
        return carry

    lax.fori_loop(0, size // GROUP, group, 0)
    lax.fori_loop(0, (size - whole + 1) // 2, pair, 0)

    def finish(i, carry):
        k = chosen[i]
        pltpu.make_async_copy(grads.at[k], patch_grads.at[k], out_sems.at[k]).wait()
        return carry

    lax.fori_loop(0, size, finish, 0)


def early_kernel(counts, offsets, tile, amps, probe, forward, inverse, patch_grads, probe_total, *scratch):
    extended, sem = scratch[0], scratch[-2]
    copies = tile_copies(tile, extended, sem) + [
        pltpu.make_async_copy(forward, scratch[4], sem),
        pltpu.make_async_copy(inverse, scratch[5], sem),
    ]
    probe_total[...] = jnp.zeros_like(probe_total)
    run_slots(True, counts, offsets, amps, patch_grads, probe, probe_total, scratch, copies)


def late_kernel(
    counts, offsets, sides, tile, rows_a, rows_b, amps, probe, forward, inverse, cols_a, cols_b, corners_a, corners_b,
    probe_before, patch_grads, probe_kept, probe_sent, probe_total, *scratch
):
    extended, side_sem, sem = scratch[0], scratch[-3], scratch[-2]
    scratch = scratch[:-3] + scratch[-2:]
    copies = tile_copies(tile, extended, sem) + [
        pltpu.make_async_copy(forward, scratch[4], sem),
        pltpu.make_async_copy(inverse, scratch[5], sem),
    ]
    even_row, even_col = sides[0] == 0, sides[1] == 0

    def strip_copies(above, below):
        return [
            pltpu.make_async_copy(
                source.at[:, :, pl.ds(b * PATCH, PATCH)], extended.at[:, b + 1, pl.ds(top, HALF), :], side_sem
            )
            for source, top in ((above, 0), (below, HALF + TILE))
            for b in range(TILE // PATCH)
        ]

    def start(above, below):
        for c in strip_copies(above, below):
            c.start()

    @pl.when(even_row)
    def _():
        start(rows_b, rows_a)

    @pl.when(jnp.logical_not(even_row))
    def _():
        start(rows_a, rows_b)

    probe_total[...] = probe_before[...]

    def columns(left, right, left_corners, right_corners):
        for rows, l, r in (
            (pl.ds(HALF, TILE), left[...], right[...]),
            (pl.ds(0, HALF), left_corners[:HALF, :], right_corners[:HALF, :]),
            (pl.ds(HALF + TILE, HALF), left_corners[HALF:, :], right_corners[HALF:, :]),
        ):
            extended[0, 0, rows, :] = pltpu.roll(l, HALF, 1)
            extended[1, 0, rows, :] = l
            extended[0, BLOCKS - 1, rows, :] = r
            extended[1, BLOCKS - 1, rows, :] = pltpu.roll(r, HALF, 1)

    @pl.when(even_col)
    def _():
        columns(cols_b, cols_a, corners_b, corners_a)

    @pl.when(jnp.logical_not(even_col))
    def _():
        columns(cols_a, cols_b, corners_a, corners_b)

    run_slots(
        False, counts, offsets, amps, patch_grads, probe, probe_total, scratch, copies, strip_copies(rows_a, rows_b)
    )
    half = MODES // 2
    put_by_side(even_col, probe_kept, probe_sent, probe_total[:half], probe_total[half:])


def put_by_side(even, a, b, after, before):
    @pl.when(even)
    def _():
        a[...] = after
        b[...] = before

    @pl.when(jnp.logical_not(even))
    def _():
        a[...] = before
        b[...] = after


def pack_kernel(sides, tile, cols_a, cols_b, first, last, sem):
    copies = [
        pltpu.make_async_copy(tile.at[:, :, pl.ds(0, PATCH)], first, sem),
        pltpu.make_async_copy(tile.at[:, :, pl.ds(TILE - PATCH, PATCH)], last, sem),
    ]
    for c in copies:
        c.start()
    for c in copies:
        c.wait()
    low = lane_iota(TILE) < HALF
    put_by_side(
        sides[1] == 0,
        cols_a,
        cols_b,
        jnp.where(low, pltpu.roll(last[0], HALF, 1), last[1]),
        jnp.where(low, first[0], pltpu.roll(first[1], HALF, 1)),
    )


def pack_corners_kernel(sides, rows_a, rows_b, corners_a, corners_b, first, last, sem):
    even_row = sides[0] == 0
    copies = []
    for i, source in enumerate((rows_a, rows_b)):
        copies.append(pltpu.make_async_copy(source.at[:, :, pl.ds(0, PATCH)], first.at[i], sem))
        copies.append(pltpu.make_async_copy(source.at[:, :, pl.ds(TILE - PATCH, PATCH)], last.at[i], sem))
    for c in copies:
        c.start()
    for c in copies:
        c.wait()
    low = lane_iota(HALF) < HALF
    for i in range(2):
        l = jnp.where(even_row, first[1 - i], first[i])
        r = jnp.where(even_row, last[1 - i], last[i])
        rows = pl.ds(i * HALF, HALF)
        put_by_side(
            sides[1] == 0,
            corners_a.at[rows, :],
            corners_b.at[rows, :],
            jnp.where(low, pltpu.roll(r[0], HALF, 1), r[1]),
            jnp.where(low, l[0], pltpu.roll(l[1], HALF, 1)),
        )


def deposit_kernel(
    counts, offsets, sides, early_grads, late_grads, inner, top, bottom, cols_a, cols_b, total, held, sems, out_sem
):
    n = PATCH
    live, first = early_slots(counts, offsets)

    def fetch(k, seen):
        inside = is_inside(offsets, k)
        is_early = inside & (seen < first)

        @pl.when(is_early)
        def _():
            pltpu.make_async_copy(early_grads.at[k], held.at[k], sems.at[k]).start()

        @pl.when(jnp.logical_not(is_early))
        def _():
            pltpu.make_async_copy(late_grads.at[k], held.at[k], sems.at[k]).start()

        return seen + jnp.where(inside, 1, 0)

    lax.fori_loop(0, live, fetch, 0)
    total[...] = jnp.zeros_like(total)
    lane = lane_iota(n)

    def turned(k):
        lead = (offsets[0, 0, 1, k] + n) % n
        pltpu.make_async_copy(early_grads.at[k], held.at[k], sems.at[k]).wait()
        return [pltpu.roll(held[k, p], lead, 1) for p in range(2)]

    def add(k, parts):
        row = offsets[0, 0, 0, k] + HALF
        col = offsets[0, 0, 1, k] + n
        block = col // n
        lead = col - block * n
        rows = pl.ds(row, n)
        old = [[total[p, block + i, rows, :] for i in range(2)] for p in range(2)]
        for p in range(2):
            total[p, block, rows, :] = old[p][0] + jnp.where(lane >= lead, parts[p], 0.0)
            total[p, block + 1, rows, :] = old[p][1] + jnp.where(lane < lead, parts[p], 0.0)

    def add_two(j, carry):
        one, two = turned(2 * j), turned(2 * j + 1)
        add(2 * j, one)
        add(2 * j + 1, two)
        return carry

    lax.fori_loop(0, live // 2, add_two, 0)

    @pl.when(live % 2 == 1)
    def _():
        add(live - 1, turned(live - 1))

    copies = []
    for start, rows, out in ((0, HALF, top), (HALF, TILE, inner), (HALF + TILE, HALF, bottom)):
        for b in range(TILE // n):
            near, far = total.at[:, b + 1, pl.ds(start, rows), :], out.at[:, :, pl.ds(b * n, n)]
            copies.append(pltpu.make_async_copy(near, far, out_sem))
    for c in copies:
        c.start()
    low = lane_iota(EXT) < HALF
    put_by_side(
        sides[1] == 0,
        cols_a,
        cols_b,
        jnp.where(low, total[0, BLOCKS - 1], pltpu.roll(total[1, BLOCKS - 1], HALF, 1)),
        jnp.where(low, pltpu.roll(total[0, 0], HALF, 1), total[1, 0]),
    )
    for c in copies:
        c.wait()


def side_terms(even_col, a, b):
    low = lane_iota(a.shape[0]) < HALF
    from_left, from_right = jnp.where(even_col, b, a), jnp.where(even_col, a, b)
    first = (jnp.where(low, from_left, 0.0), jnp.where(low, pltpu.roll(from_left, HALF, 1), 0.0))
    last = (jnp.where(low, 0.0, pltpu.roll(from_right, HALF, 1)), jnp.where(low, 0.0, from_right))
    return first, last


def edges_kernel(sides, top, bottom, cols_a, cols_b, rows_a, rows_b):
    end = TILE - PATCH
    sent = []
    for part, rows in ((top, slice(0, HALF)), (bottom, slice(HALF + TILE, EXT))):
        first, last = side_terms(sides[1] == 0, cols_a[rows, :], cols_b[rows, :])
        sent.append(
            [
                jnp.concatenate([part[p, :, :PATCH] + first[p], part[p, :, PATCH:end], part[p, :, end:] + last[p]], 1)
                for p in range(2)
            ]
        )
    for p in range(2):
        put_by_side(sides[0] == 0, rows_a.at[p], rows_b.at[p], sent[1][p], sent[0][p])


def merge_kernel(sides, inner, cols_a, cols_b, rows_a, rows_b, out, left, right, top, bottom, sems):
    end = TILE - PATCH
    regions = (
        (out.at[:, :, pl.ds(0, PATCH)], left),
        (out.at[:, :, pl.ds(end, PATCH)], right),
        (out.at[:, pl.ds(0, HALF), pl.ds(PATCH, TILE - 2 * PATCH)], top),
        (out.at[:, pl.ds(TILE - HALF, HALF), pl.ds(PATCH, TILE - 2 * PATCH)], bottom),
    )
    loads = [pltpu.make_async_copy(far, near, sems.at[i]) for i, (far, near) in enumerate(regions)]
    for c in loads:
        c.start()
    a, b = rows_a[...], rows_b[...]
    above, below = jnp.where(sides[0] == 0, b, a), jnp.where(sides[0] == 0, a, b)
    own = slice(HALF, HALF + TILE)
    terms = side_terms(sides[1] == 0, cols_a[own, :], cols_b[own, :])
    for c in loads:
        c.wait()
    middle = slice(PATCH, end)
    for p in range(2):
        for near, term, lanes in ((left, terms[0][p], slice(0, PATCH)), (right, terms[1][p], slice(end, TILE))):
            near[p] += term
            near[p, :HALF, :] += above[p, :, lanes]
            near[p, TILE - HALF :, :] += below[p, :, lanes]
        top[p] += above[p, :, middle]
        bottom[p] += below[p, :, middle]
    stores = [pltpu.make_async_copy(near, far, sems.at[i]) for i, (far, near) in enumerate(regions)]
    for c in stores:
        c.start()
    for c in stores:
        c.wait()


VMEM = pl.BlockSpec(memory_space=pltpu.VMEM)
SMEM = pl.BlockSpec(memory_space=pltpu.SMEM)
HBM = pl.BlockSpec(memory_space=pltpu.HBM)


def call(kernel, in_specs, out_specs, out_shapes, scratch, *args, aliases=None, limit=62):
    return pl.pallas_call(
        kernel,
        in_specs=in_specs,
        out_specs=out_specs,
        out_shape=[jax.ShapeDtypeStruct(s, jnp.float32) for s in out_shapes],
        scratch_shapes=scratch,
        input_output_aliases=aliases or {},
        compiler_params=pltpu.CompilerParams(vmem_limit_bytes=limit * 2**20),
    )(*args)


def swap(value, axes, size, first):
    pairs = [(i, i + 1) for i in range(first, size - 1, 2)]
    return lax.ppermute(value, axes, pairs + [(j, i) for i, j in pairs])


def double(x, axis):
    other, me = swap(x, axis, 2, 0), lax.axis_index(axis)
    return jnp.where(me == 0, jnp.concatenate([x, other], 0), jnp.concatenate([other, x], 0))


def deal(x, axes, sizes):
    count = math.prod(sizes[a] for a in axes)
    return lax.all_to_all(x.reshape(count, -1, PATCH), axes, 0, 0, tiled=True)


def spread(x, axes, sizes):
    count = math.prod(sizes[a] for a in axes)
    return lax.all_to_all(jnp.broadcast_to(x[None], (count, *x.shape)), axes, 0, 0, tiled=True)


def per_device(sizes, tile, probe, amplitudes, offsets, counts):
    rows, cols = sizes["zh"] * sizes["x"], sizes["y"] * sizes["zl"] * sizes["core"]
    forward, inverse = [jnp.asarray(t) for t in dft_tables(PATCH)]
    offsets = offsets.transpose(0, 1, 3, 2)
    amps = amplitudes.reshape(SLOTS, PATCH, PATCH)
    odd_row, odd_col = lax.axis_index(ROW) % 2, lax.axis_index(COL) % 2
    sides = jnp.stack([odd_row, odd_col]).astype(jnp.int32)
    wide = 2 * PATCH
    slot_scratch = [
        pltpu.VMEM((2, BLOCKS, EXT, PATCH), jnp.float32),
        pltpu.VMEM((SLOTS, PATCH, PATCH), jnp.float32),
        pltpu.VMEM((MODES, 2, PATCH, PATCH), jnp.float32),
        pltpu.VMEM((SLOTS + 1, 2, PATCH, PATCH), jnp.float32),
        pltpu.VMEM((2, wide, wide), jnp.bfloat16),
        pltpu.VMEM((2, wide, wide), jnp.bfloat16),
        pltpu.SMEM((SLOTS + 1,), jnp.int32),
        pltpu.SemaphoreType.DMA,
        pltpu.SemaphoreType.DMA((SLOTS,)),
    ]
    grads_shape, probe_shape = (SLOTS, 2, PATCH, PATCH), (MODES, 2, PATCH, PATCH)
    strip, column = (2, HALF, TILE), (TILE, PATCH)
    block = pltpu.VMEM((2, TILE, PATCH), jnp.float32)
    low, high = 0, TILE - HALF
    after = lax.dynamic_slice_in_dim(tile, jnp.where(odd_row == 0, high, low), HALF, 1)
    before = lax.dynamic_slice_in_dim(tile, jnp.where(odd_row == 0, low, high), HALF, 1)
    rows_b = swap(before, ROW, rows, 1)
    rows_a = swap(after, ROW, rows, 0)
    cols_a, cols_b = call(
        pack_kernel, [SMEM, HBM], [VMEM] * 2, [column] * 2, [block, block, pltpu.SemaphoreType.DMA], sides, tile, limit=16
    )
    cols_b = swap(cols_b, COL, cols, 1)
    cols_a = swap(cols_a, COL, cols, 0)
    early_grads, probe_early = call(
        early_kernel, [SMEM] * 2 + [HBM] * 5, [HBM, VMEM], [grads_shape, probe_shape], slot_scratch,
        counts, offsets, tile, amps, probe, forward, inverse
    )
    rows_a, rows_b, probe_early = lax.optimization_barrier((rows_a, rows_b, probe_early))
    piece = pltpu.VMEM((2, 2, HALF, PATCH), jnp.float32)
    corners_a, corners_b = call(
        pack_corners_kernel, [SMEM] + [HBM] * 2, [VMEM] * 2, [(PATCH, PATCH)] * 2, [piece, piece, pltpu.SemaphoreType.DMA],
        sides, rows_a, rows_b, limit=16
    )
    corners_b = swap(corners_b, COL, cols, 1)
    corners_a = swap(corners_a, COL, cols, 0)
    half_shape = (MODES // 2, 2, PATCH, PATCH)
    late_scratch = [pltpu.VMEM(probe_shape, jnp.float32)] + slot_scratch[:-2] + [pltpu.SemaphoreType.DMA] + slot_scratch[-2:]
    late_grads, probe_kept, probe_sent = call(
        late_kernel, [SMEM] * 3 + [HBM] * 7 + [VMEM] * 5, [HBM, VMEM, VMEM], [grads_shape, half_shape, half_shape], late_scratch,
        counts, offsets, sides, tile, rows_a, rows_b, amps, probe, forward, inverse, cols_a, cols_b, corners_a, corners_b, probe_early
    )

    sums = (probe_kept + swap(probe_sent, "core", 2, 0)).reshape(-1, PATCH)
    inner, top, bottom, cols_a, cols_b = call(
        deposit_kernel, [SMEM] * 3 + [HBM] * 2, [HBM] * 3 + [VMEM] * 2,
        [(2, TILE, TILE), strip, strip, (EXT, PATCH), (EXT, PATCH)],
        [
            pltpu.VMEM((2, BLOCKS, EXT, PATCH), jnp.float32),
            pltpu.VMEM(grads_shape, jnp.float32),
            pltpu.SemaphoreType.DMA((SLOTS,)),
            pltpu.SemaphoreType.DMA,
        ],
        counts, offsets, sides, early_grads, late_grads
    )
    cols_b = swap(cols_b, COL, cols, 1)
    cols_a = swap(cols_a, COL, cols, 0)
    plane, line = ("x", "y"), ("zh", "zl")
    sums = jnp.sum(deal(sums, plane, sizes), 0)
    rows_a, rows_b = call(
        edges_kernel, [SMEM] + [VMEM] * 4, [VMEM] * 2, [strip] * 2, [], sides, top, bottom, cols_a, cols_b, limit=16
    )
    sums = jnp.sum(spread(sums, line, sizes), 0)
    sums, rows_a, rows_b = lax.optimization_barrier((sums, rows_a, rows_b))
    rows_b = swap(rows_b, ROW, rows, 1)
    rows_a = swap(rows_a, ROW, rows, 0)
    sums = spread(sums, plane, sizes).reshape(-1, PATCH)
    sums, rows_a, rows_b = lax.optimization_barrier((sums, rows_a, rows_b))
    end = pltpu.VMEM((2, HALF, TILE - 2 * PATCH), jnp.float32)
    (object_grad,) = call(
        merge_kernel, [SMEM, HBM] + [VMEM] * 4, [HBM], [(2, TILE, TILE)],
        [block, block, end, end, pltpu.SemaphoreType.DMA((4,))],
        sides, inner, cols_a, cols_b, rows_a, rows_b, aliases={1: 0}, limit=16
    )
    factor = 1.0 / math.sqrt(rows * cols * SLOTS)
    probe_grad = (double(sums, "core") * factor).reshape(probe_shape)
    return object_grad, probe_grad


def solution(mesh):
    sizes = {"zh": 4, "x": 4, "y": 4, "zl": 2, "core": 2}
    fine = Mesh(mesh.devices.reshape(tuple(sizes.values())), tuple(sizes))
    return jax.shard_map(
        functools.partial(per_device, sizes),
        mesh=fine,
        in_specs=(P(None, ROW, COL), P(), P(ROW, COL), P(ROW, COL), P(ROW, COL)),
        out_specs=(P(None, ROW, COL), P()),
        check_vma=False,
    )
```

```python
import functools
import math

import jax
import jax.numpy as jnp
import ml_dtypes
import numpy as np
from jax import lax
from jax.experimental import pallas as pl
from jax.experimental.pallas import tpu as pltpu
from jax.sharding import Mesh
from jax.sharding import PartitionSpec as P

PATCH = 128
MODES = 4
TILE = 512
SLOTS = 16
HALF = 64
EXT = TILE + 2 * HALF
BLOCKS = 6
GROUP = 4

ROW = ("zh", "x")
COL = ("y", "zl", "core")


def split_table(table):
    high = table.astype(np.float32).astype(ml_dtypes.bfloat16)
    low = (table - high.astype(np.float64)).astype(np.float32).astype(ml_dtypes.bfloat16)
    return high, low


def dft_tables(n):
    i = np.arange(n)
    angles = (np.outer(i, i) % n) * (2 * math.pi / n)
    cos, sin = np.cos(angles) / math.sqrt(n), -np.sin(angles) / math.sqrt(n)
    forward = np.block([[cos, sin], [-sin, cos]])
    fh, fl = split_table(forward)
    ih, il = split_table(forward.T)
    return np.stack([fh, fl]), np.stack([ih, il])


def split(x):
    high = x.astype(jnp.bfloat16)
    return high, (x - high.astype(jnp.float32)).astype(jnp.bfloat16)


def dot(a, b):
    return jnp.dot(a, b, preferred_element_type=jnp.float32)


def right_dft(x, table):
    high, low = split(x)
    return dot(high, table[0]) + dot(low, table[0]) + dot(high, table[1])


def left_dft(table, x):
    high, low = split(x)
    return dot(table[0], high) + dot(table[1], high) + dot(table[0], low)


def to_cols(y):
    n = PATCH
    return jnp.concatenate(
        [jnp.concatenate([y[m * n : (m + 1) * n, p * n : (p + 1) * n] for m in range(MODES)], 1) for p in range(2)], 0
    )


def to_rows(z):
    n = PATCH
    return jnp.concatenate(
        [jnp.concatenate([z[p * n : (p + 1) * n, m * n : (m + 1) * n] for p in range(2)], 1) for m in range(MODES)], 0
    )


def lane_iota(rows):
    return lax.broadcasted_iota(jnp.int32, (rows, PATCH), 1)


def is_inside(offsets, k):
    r, c = offsets[0, 0, 0, k], offsets[0, 0, 1, k]
    top = TILE - PATCH
    return (r >= 0) & (r <= top) & (c >= 0) & (c <= top)


def early_slots(counts, offsets):
    live = counts[0, 0]

    def tally(k, total):
        return total + jnp.where(is_inside(offsets, k) & (k < live), 1, 0)

    inside = lax.fori_loop(0, SLOTS, tally, 0)
    return live, inside // 2 * 2


def choose_slots(counts, offsets, chosen, early):
    live, first = early_slots(counts, offsets)

    def pick(k, state):
        seen, size = state
        inner = is_inside(offsets, k)
        is_early = inner & (seen < first)
        chosen[size] = k
        take = (is_early == early) & (k < live)
        seen = seen + jnp.where(inner, 1, 0)
        return seen, size + jnp.where(take, 1, 0)

    _, size = lax.fori_loop(0, SLOTS, pick, (0, 0))
    return size


def slot_work(k, out_slot, scale, offsets, extended, amplitudes, probe, tables, patch_grads, probe_total):
    forward, inverse = tables
    n = PATCH
    row = offsets[0, 0, 0, k] + HALF
    col = offsets[0, 0, 1, k] + PATCH
    block = col // n
    lead = col - block * n
    turn = jnp.where(lead == 0, 0, n - lead)
    lane = lane_iota(n)
    parts = []
    for p in range(2):
        a = pltpu.roll(extended[p, block, pl.ds(row, n), :], turn, 1)
        b = pltpu.roll(extended[p, block + 1, pl.ds(row, n), :], turn, 1)
        parts.append(jnp.where(lane < n - lead, a, b))
    obj_r, obj_i = parts
    waves = []
    for m in range(MODES):
        pr, pi = probe[m, 0], probe[m, 1]
        waves.append(jnp.concatenate([pr * obj_r - pi * obj_i, pr * obj_i + pi * obj_r], 1))
    far = left_dft(inverse, to_cols(right_dft(jnp.concatenate(waves, 0), forward)))
    power = far * far
    power = power[:n] + power[n:]
    intensity = power[:, :n] + power[:, n : 2 * n] + power[:, 2 * n : 3 * n] + power[:, 3 * n :]
    measured = amplitudes[k]
    residual = (intensity - measured * measured) * scale
    weighted = far * jnp.concatenate([jnp.concatenate([residual] * MODES, 1)] * 2, 0)
    back = right_dft(to_rows(left_dft(forward, weighted)), inverse)
    total_r = total_i = None
    for m in range(MODES):
        gr, gi = back[m * n : (m + 1) * n, :n], back[m * n : (m + 1) * n, n:]
        pr, pi = probe[m, 0], probe[m, 1]
        tr, ti = pr * gr + pi * gi, pr * gi - pi * gr
        total_r, total_i = (tr, ti) if m == 0 else (total_r + tr, total_i + ti)
        probe_total[m, 0] += obj_r * gr + obj_i * gi
        probe_total[m, 1] += obj_r * gi - obj_i * gr
    patch_grads[out_slot, 0] = total_r
    patch_grads[out_slot, 1] = total_i


def tile_copies(tile, extended, sem):
    return [
        pltpu.make_async_copy(
            tile.at[:, :, pl.ds(b * PATCH, PATCH)], extended.at[:, b + 1, pl.ds(HALF, TILE), :], sem
        )
        for b in range(TILE // PATCH)
    ]


def run_slots(early, counts, offsets, amps, patch_grads, probe_in, probe_total, scratch, copies, others=()):
    extended, measured, probe, grads, forward, inverse, chosen, sem, out_sems = scratch
    copies = copies + [pltpu.make_async_copy(amps, measured, sem), pltpu.make_async_copy(probe_in, probe, sem)]
    for c in copies:
        c.start()
    size = choose_slots(counts, offsets, chosen, early)
    for c in [*copies, *others]:
        c.wait()

    def step(first, count):
        for u in range(count):
            i = first + u
            on = i < size
            k = jnp.where(on, chosen[jnp.minimum(i, SLOTS - 1)], 0)
            out = jnp.where(on, k, SLOTS)
            scale = jnp.where(on, 2.0, 0.0)
            slot_work(k, out, scale, offsets, extended, measured, probe, (forward, inverse), grads, probe_total)
        for u in range(count):
            i = first + u

            @pl.when(i < size)
            def _():
                k = chosen[i]
                pltpu.make_async_copy(grads.at[k], patch_grads.at[k], out_sems.at[k]).start()

    whole = size // GROUP * GROUP

    def group(j, carry):
        step(j * GROUP, GROUP)
        return carry

    def pair(j, carry):
        step(whole + j * 2, 2)
        return carry

    lax.fori_loop(0, size // GROUP, group, 0)
    lax.fori_loop(0, (size - whole + 1) // 2, pair, 0)

    def finish(i, carry):
        k = chosen[i]
        pltpu.make_async_copy(grads.at[k], patch_grads.at[k], out_sems.at[k]).wait()
        return carry

    lax.fori_loop(0, size, finish, 0)


def early_kernel(counts, offsets, tile, amps, probe, forward, inverse, patch_grads, probe_total, *scratch):
    extended, sem = scratch[0], scratch[-2]
    copies = tile_copies(tile, extended, sem) + [
        pltpu.make_async_copy(forward, scratch[4], sem),
        pltpu.make_async_copy(inverse, scratch[5], sem),
    ]
    probe_total[...] = jnp.zeros_like(probe_total)
    run_slots(True, counts, offsets, amps, patch_grads, probe, probe_total, scratch, copies)


def late_kernel(
    counts, offsets, sides, tile, rows_a, rows_b, amps, probe, forward, inverse, cols_a, cols_b, corners_a, corners_b,
    probe_before, patch_grads, probe_kept, probe_sent, probe_total, *scratch
):
    extended, side_sem, sem = scratch[0], scratch[-3], scratch[-2]
    scratch = scratch[:-3] + scratch[-2:]
    copies = tile_copies(tile, extended, sem) + [
        pltpu.make_async_copy(forward, scratch[4], sem),
        pltpu.make_async_copy(inverse, scratch[5], sem),
    ]
    even_row, even_col = sides[0] == 0, sides[1] == 0

    def strip_copies(above, below):
        return [
            pltpu.make_async_copy(
                source.at[:, :, pl.ds(b * PATCH, PATCH)], extended.at[:, b + 1, pl.ds(top, HALF), :], side_sem
            )
            for source, top in ((above, 0), (below, HALF + TILE))
            for b in range(TILE // PATCH)
        ]

    def start(above, below):
        for c in strip_copies(above, below):
            c.start()

    @pl.when(even_row)
    def _():
        start(rows_b, rows_a)

    @pl.when(jnp.logical_not(even_row))
    def _():
        start(rows_a, rows_b)

    probe_total[...] = probe_before[...]

    def columns(left, right, left_corners, right_corners):
        for rows, l, r in (
            (pl.ds(HALF, TILE), left[...], right[...]),
            (pl.ds(0, HALF), left_corners[:HALF, :], right_corners[:HALF, :]),
            (pl.ds(HALF + TILE, HALF), left_corners[HALF:, :], right_corners[HALF:, :]),
        ):
            extended[0, 0, rows, :] = pltpu.roll(l, HALF, 1)
            extended[1, 0, rows, :] = l
            extended[0, BLOCKS - 1, rows, :] = r
            extended[1, BLOCKS - 1, rows, :] = pltpu.roll(r, HALF, 1)

    @pl.when(even_col)
    def _():
        columns(cols_b, cols_a, corners_b, corners_a)

    @pl.when(jnp.logical_not(even_col))
    def _():
        columns(cols_a, cols_b, corners_a, corners_b)

    run_slots(
        False, counts, offsets, amps, patch_grads, probe, probe_total, scratch, copies, strip_copies(rows_a, rows_b)
    )
    half = MODES // 2
    put_by_side(even_col, probe_kept, probe_sent, probe_total[:half], probe_total[half:])


def put_by_side(even, a, b, after, before):
    @pl.when(even)
    def _():
        a[...] = after
        b[...] = before

    @pl.when(jnp.logical_not(even))
    def _():
        a[...] = before
        b[...] = after


def pack_kernel(sides, tile, cols_a, cols_b, first, last, sem):
    copies = [
        pltpu.make_async_copy(tile.at[:, :, pl.ds(0, PATCH)], first, sem),
        pltpu.make_async_copy(tile.at[:, :, pl.ds(TILE - PATCH, PATCH)], last, sem),
    ]
    for c in copies:
        c.start()
    for c in copies:
        c.wait()
    low = lane_iota(TILE) < HALF
    put_by_side(
        sides[1] == 0,
        cols_a,
        cols_b,
        jnp.where(low, pltpu.roll(last[0], HALF, 1), last[1]),
        jnp.where(low, first[0], pltpu.roll(first[1], HALF, 1)),
    )


def pack_corners_kernel(sides, rows_a, rows_b, corners_a, corners_b, first, last, sem):
    even_row = sides[0] == 0
    copies = []
    for i, source in enumerate((rows_a, rows_b)):
        copies.append(pltpu.make_async_copy(source.at[:, :, pl.ds(0, PATCH)], first.at[i], sem))
        copies.append(pltpu.make_async_copy(source.at[:, :, pl.ds(TILE - PATCH, PATCH)], last.at[i], sem))
    for c in copies:
        c.start()
    for c in copies:
        c.wait()
    low = lane_iota(HALF) < HALF
    for i in range(2):
        l = jnp.where(even_row, first[1 - i], first[i])
        r = jnp.where(even_row, last[1 - i], last[i])
        rows = pl.ds(i * HALF, HALF)
        put_by_side(
            sides[1] == 0,
            corners_a.at[rows, :],
            corners_b.at[rows, :],
            jnp.where(low, pltpu.roll(r[0], HALF, 1), r[1]),
            jnp.where(low, l[0], pltpu.roll(l[1], HALF, 1)),
        )


def deposit_kernel(
    counts, offsets, sides, early_grads, late_grads, inner, top, bottom, cols_a, cols_b, total, held, sems, out_sem
):
    n = PATCH
    live, first = early_slots(counts, offsets)

    def fetch(k, seen):
        inside = is_inside(offsets, k)
        is_early = inside & (seen < first)

        @pl.when(is_early)
        def _():
            pltpu.make_async_copy(early_grads.at[k], held.at[k], sems.at[k]).start()

        @pl.when(jnp.logical_not(is_early))
        def _():
            pltpu.make_async_copy(late_grads.at[k], held.at[k], sems.at[k]).start()

        return seen + jnp.where(inside, 1, 0)

    lax.fori_loop(0, live, fetch, 0)
    total[...] = jnp.zeros_like(total)
    lane = lane_iota(n)

    def turned(k):
        lead = (offsets[0, 0, 1, k] + n) % n
        pltpu.make_async_copy(early_grads.at[k], held.at[k], sems.at[k]).wait()
        return [pltpu.roll(held[k, p], lead, 1) for p in range(2)]

    def add(k, parts):
        row = offsets[0, 0, 0, k] + HALF
        col = offsets[0, 0, 1, k] + n
        block = col // n
        lead = col - block * n
        rows = pl.ds(row, n)
        old = [[total[p, block + i, rows, :] for i in range(2)] for p in range(2)]
        for p in range(2):
            total[p, block, rows, :] = old[p][0] + jnp.where(lane >= lead, parts[p], 0.0)
            total[p, block + 1, rows, :] = old[p][1] + jnp.where(lane < lead, parts[p], 0.0)

    def add_two(j, carry):
        one, two = turned(2 * j), turned(2 * j + 1)
        add(2 * j, one)
        add(2 * j + 1, two)
        return carry

    lax.fori_loop(0, live // 2, add_two, 0)

    @pl.when(live % 2 == 1)
    def _():
        add(live - 1, turned(live - 1))

    copies = []
    for start, rows, out in ((0, HALF, top), (HALF, TILE, inner), (HALF + TILE, HALF, bottom)):
        for b in range(TILE // n):
            near, far = total.at[:, b + 1, pl.ds(start, rows), :], out.at[:, :, pl.ds(b * n, n)]
            copies.append(pltpu.make_async_copy(near, far, out_sem))
    for c in copies:
        c.start()
    low = lane_iota(EXT) < HALF
    put_by_side(
        sides[1] == 0,
        cols_a,
        cols_b,
        jnp.where(low, total[0, BLOCKS - 1], pltpu.roll(total[1, BLOCKS - 1], HALF, 1)),
        jnp.where(low, pltpu.roll(total[0, 0], HALF, 1), total[1, 0]),
    )
    for c in copies:
        c.wait()


def side_terms(even_col, a, b):
    low = lane_iota(a.shape[0]) < HALF
    from_left, from_right = jnp.where(even_col, b, a), jnp.where(even_col, a, b)
    first = (jnp.where(low, from_left, 0.0), jnp.where(low, pltpu.roll(from_left, HALF, 1), 0.0))
    last = (jnp.where(low, 0.0, pltpu.roll(from_right, HALF, 1)), jnp.where(low, 0.0, from_right))
    return first, last


def edges_kernel(sides, top, bottom, cols_a, cols_b, rows_a, rows_b):
    end = TILE - PATCH
    sent = []
    for part, rows in ((top, slice(0, HALF)), (bottom, slice(HALF + TILE, EXT))):
        first, last = side_terms(sides[1] == 0, cols_a[rows, :], cols_b[rows, :])
        sent.append(
            [
                jnp.concatenate([part[p, :, :PATCH] + first[p], part[p, :, PATCH:end], part[p, :, end:] + last[p]], 1)
                for p in range(2)
            ]
        )
    for p in range(2):
        put_by_side(sides[0] == 0, rows_a.at[p], rows_b.at[p], sent[1][p], sent[0][p])


def merge_kernel(sides, inner, cols_a, cols_b, rows_a, rows_b, out, left, right, top, bottom, sems):
    end = TILE - PATCH
    regions = (
        (out.at[:, :, pl.ds(0, PATCH)], left),
        (out.at[:, :, pl.ds(end, PATCH)], right),
        (out.at[:, pl.ds(0, HALF), pl.ds(PATCH, TILE - 2 * PATCH)], top),
        (out.at[:, pl.ds(TILE - HALF, HALF), pl.ds(PATCH, TILE - 2 * PATCH)], bottom),
    )
    loads = [pltpu.make_async_copy(far, near, sems.at[i]) for i, (far, near) in enumerate(regions)]
    for c in loads:
        c.start()
    a, b = rows_a[...], rows_b[...]
    above, below = jnp.where(sides[0] == 0, b, a), jnp.where(sides[0] == 0, a, b)
    own = slice(HALF, HALF + TILE)
    terms = side_terms(sides[1] == 0, cols_a[own, :], cols_b[own, :])
    for c in loads:
        c.wait()
    middle = slice(PATCH, end)
    for p in range(2):
        for near, term, lanes in ((left, terms[0][p], slice(0, PATCH)), (right, terms[1][p], slice(end, TILE))):
            near[p] += term
            near[p, :HALF, :] += above[p, :, lanes]
            near[p, TILE - HALF :, :] += below[p, :, lanes]
        top[p] += above[p, :, middle]
        bottom[p] += below[p, :, middle]
    stores = [pltpu.make_async_copy(near, far, sems.at[i]) for i, (far, near) in enumerate(regions)]
    for c in stores:
        c.start()
    for c in stores:
        c.wait()


VMEM = pl.BlockSpec(memory_space=pltpu.VMEM)
SMEM = pl.BlockSpec(memory_space=pltpu.SMEM)
HBM = pl.BlockSpec(memory_space=pltpu.HBM)


def call(kernel, in_specs, out_specs, out_shapes, scratch, *args, aliases=None, limit=62):
    return pl.pallas_call(
        kernel,
        in_specs=in_specs,
        out_specs=out_specs,
        out_shape=[jax.ShapeDtypeStruct(s, jnp.float32) for s in out_shapes],
        scratch_shapes=scratch,
        input_output_aliases=aliases or {},
        compiler_params=pltpu.CompilerParams(vmem_limit_bytes=limit * 2**20),
    )(*args)


def swap(value, axes, size, first):
    pairs = [(i, i + 1) for i in range(first, size - 1, 2)]
    return lax.ppermute(value, axes, pairs + [(j, i) for i, j in pairs])


def double(x, axis):
    other, me = swap(x, axis, 2, 0), lax.axis_index(axis)
    return jnp.where(me == 0, jnp.concatenate([x, other], 0), jnp.concatenate([other, x], 0))


def deal(x, axes, sizes):
    count = math.prod(sizes[a] for a in axes)
    return lax.all_to_all(x.reshape(count, -1, PATCH), axes, 0, 0, tiled=True)


def spread(x, axes, sizes):
    count = math.prod(sizes[a] for a in axes)
    return lax.all_to_all(jnp.broadcast_to(x[None], (count, *x.shape)), axes, 0, 0, tiled=True)


def per_device(sizes, tile, probe, amplitudes, offsets, counts):
    rows, cols = sizes["zh"] * sizes["x"], sizes["y"] * sizes["zl"] * sizes["core"]
    forward, inverse = [jnp.asarray(t) for t in dft_tables(PATCH)]
    offsets = offsets.transpose(0, 1, 3, 2)
    amps = amplitudes.reshape(SLOTS, PATCH, PATCH)
    odd_row, odd_col = lax.axis_index(ROW) % 2, lax.axis_index(COL) % 2
    sides = jnp.stack([odd_row, odd_col]).astype(jnp.int32)
    wide = 2 * PATCH
    slot_scratch = [
        pltpu.VMEM((2, BLOCKS, EXT, PATCH), jnp.float32),
        pltpu.VMEM((SLOTS, PATCH, PATCH), jnp.float32),
        pltpu.VMEM((MODES, 2, PATCH, PATCH), jnp.float32),
        pltpu.VMEM((SLOTS + 1, 2, PATCH, PATCH), jnp.float32),
        pltpu.VMEM((2, wide, wide), jnp.bfloat16),
        pltpu.VMEM((2, wide, wide), jnp.bfloat16),
        pltpu.SMEM((SLOTS + 1,), jnp.int32),
        pltpu.SemaphoreType.DMA,
        pltpu.SemaphoreType.DMA((SLOTS,)),
    ]
    grads_shape, probe_shape = (SLOTS, 2, PATCH, PATCH), (MODES, 2, PATCH, PATCH)
    strip, column = (2, HALF, TILE), (TILE, PATCH)
    block = pltpu.VMEM((2, TILE, PATCH), jnp.float32)
    low, high = 0, TILE - HALF
    after = lax.dynamic_slice_in_dim(tile, jnp.where(odd_row == 0, high, low), HALF, 1)
    before = lax.dynamic_slice_in_dim(tile, jnp.where(odd_row == 0, low, high), HALF, 1)
    rows_b = swap(before, ROW, rows, 1)
    rows_a = swap(after, ROW, rows, 0)
    cols_a, cols_b = call(
        pack_kernel, [SMEM, HBM], [VMEM] * 2, [column] * 2, [block, block, pltpu.SemaphoreType.DMA], sides, tile, limit=16
    )
    cols_b = swap(cols_b, COL, cols, 1)
    cols_a = swap(cols_a, COL, cols, 0)
    early_grads, probe_early = call(
        early_kernel, [SMEM] * 2 + [HBM] * 5, [HBM, VMEM], [grads_shape, probe_shape], slot_scratch,
        counts, offsets, tile, amps, probe, forward, inverse
    )
    rows_a, rows_b, probe_early = lax.optimization_barrier((rows_a, rows_b, probe_early))
    piece = pltpu.VMEM((2, 2, HALF, PATCH), jnp.float32)
    corners_a, corners_b = call(
        pack_corners_kernel, [SMEM] + [HBM] * 2, [VMEM] * 2, [(PATCH, PATCH)] * 2, [piece, piece, pltpu.SemaphoreType.DMA],
        sides, rows_a, rows_b, limit=16
    )
    corners_b = swap(corners_b, COL, cols, 1)
    corners_a = swap(corners_a, COL, cols, 0)
    half_shape = (MODES // 2, 2, PATCH, PATCH)
    late_scratch = [pltpu.VMEM(probe_shape, jnp.float32)] + slot_scratch[:-2] + [pltpu.SemaphoreType.DMA] + slot_scratch[-2:]
    late_grads, probe_kept, probe_sent = call(
        late_kernel, [SMEM] * 3 + [HBM] * 7 + [VMEM] * 5, [HBM, VMEM, VMEM], [grads_shape, half_shape, half_shape], late_scratch,
        counts, offsets, sides, tile, rows_a, rows_b, amps, probe, forward, inverse, cols_a, cols_b, corners_a, corners_b, probe_early
    )

    sums = (probe_kept + swap(probe_sent, "core", 2, 0)).reshape(-1, PATCH)
    inner, top, bottom, cols_a, cols_b = call(
        deposit_kernel, [SMEM] * 3 + [HBM] * 2, [HBM] * 3 + [VMEM] * 2,
        [(2, TILE, TILE), strip, strip, (EXT, PATCH), (EXT, PATCH)],
        [
            pltpu.VMEM((2, BLOCKS, EXT, PATCH), jnp.float32),
            pltpu.VMEM(grads_shape, jnp.float32),
            pltpu.SemaphoreType.DMA((SLOTS,)),
            pltpu.SemaphoreType.DMA,
        ],
        counts, offsets, sides, early_grads, late_grads
    )
    cols_b = swap(cols_b, COL, cols, 1)
    cols_a = swap(cols_a, COL, cols, 0)
    plane, line = ("x", "y"), ("zh", "zl")
    sums = jnp.sum(deal(sums, plane, sizes), 0)
    rows_a, rows_b = call(
        edges_kernel, [SMEM] + [VMEM] * 4, [VMEM] * 2, [strip] * 2, [], sides, top, bottom, cols_a, cols_b, limit=16
    )
    sums = jnp.sum(spread(sums, line, sizes), 0)
    rows_b = swap(rows_b, ROW, rows, 1)
    rows_a = swap(rows_a, ROW, rows, 0)
    sums = spread(sums, plane, sizes).reshape(-1, PATCH)
    sums, rows_a, rows_b = lax.optimization_barrier((sums, rows_a, rows_b))
    end = pltpu.VMEM((2, HALF, TILE - 2 * PATCH), jnp.float32)
    (object_grad,) = call(
        merge_kernel, [SMEM, HBM] + [VMEM] * 4, [HBM], [(2, TILE, TILE)],
        [block, block, end, end, pltpu.SemaphoreType.DMA((4,))],
        sides, inner, cols_a, cols_b, rows_a, rows_b, aliases={1: 0}, limit=16
    )
    factor = 1.0 / math.sqrt(rows * cols * SLOTS)
    probe_grad = (double(sums, "core") * factor).reshape(probe_shape)
    return object_grad, probe_grad


def solution(mesh):
    sizes = {"zh": 4, "x": 4, "y": 4, "zl": 2, "core": 2}
    fine = Mesh(mesh.devices.reshape(tuple(sizes.values())), tuple(sizes))
    return jax.shard_map(
        functools.partial(per_device, sizes),
        mesh=fine,
        in_specs=(P(None, ROW, COL), P(), P(ROW, COL), P(ROW, COL), P(ROW, COL)),
        out_specs=(P(None, ROW, COL), P()),
        check_vma=False,
    )
```

```python
import functools
import math

import jax
import jax.numpy as jnp
import ml_dtypes
import numpy as np
from jax import lax
from jax.experimental import pallas as pl
from jax.experimental.pallas import tpu as pltpu
from jax.sharding import Mesh
from jax.sharding import PartitionSpec as P

PATCH = 128
MODES = 4
TILE = 512
SLOTS = 16
HALF = 64
EXT = TILE + 2 * HALF
BLOCKS = 6
GROUP = 4

ROW = ("zh", "x")
COL = ("y", "zl", "core")


def split_table(table):
    high = table.astype(np.float32).astype(ml_dtypes.bfloat16)
    low = (table - high.astype(np.float64)).astype(np.float32).astype(ml_dtypes.bfloat16)
    return high, low


def dft_tables(n):
    i = np.arange(n)
    angles = (np.outer(i, i) % n) * (2 * math.pi / n)
    cos, sin = np.cos(angles) / math.sqrt(n), -np.sin(angles) / math.sqrt(n)
    forward = np.block([[cos, sin], [-sin, cos]])
    fh, fl = split_table(forward)
    ih, il = split_table(forward.T)
    return np.stack([fh, fl]), np.stack([ih, il])


def split(x):
    high = x.astype(jnp.bfloat16)
    return high, (x - high.astype(jnp.float32)).astype(jnp.bfloat16)


def dot(a, b):
    return jnp.dot(a, b, preferred_element_type=jnp.float32)


def right_dft(x, table):
    high, low = split(x)
    return dot(high, table[0]) + dot(low, table[0]) + dot(high, table[1])


def left_dft(table, x):
    high, low = split(x)
    return dot(table[0], high) + dot(table[1], high) + dot(table[0], low)


def to_cols(y):
    n = PATCH
    return jnp.concatenate(
        [jnp.concatenate([y[m * n : (m + 1) * n, p * n : (p + 1) * n] for m in range(MODES)], 1) for p in range(2)], 0
    )


def to_rows(z):
    n = PATCH
    return jnp.concatenate(
        [jnp.concatenate([z[p * n : (p + 1) * n, m * n : (m + 1) * n] for p in range(2)], 1) for m in range(MODES)], 0
    )


def lane_iota(rows):
    return lax.broadcasted_iota(jnp.int32, (rows, PATCH), 1)


def is_inside(offsets, k):
    r, c = offsets[0, 0, 0, k], offsets[0, 0, 1, k]
    top = TILE - PATCH
    return (r >= 0) & (r <= top) & (c >= 0) & (c <= top)


def early_slots(counts, offsets):
    live = counts[0, 0]

    def tally(k, total):
        return total + jnp.where(is_inside(offsets, k) & (k < live), 1, 0)

    inside = lax.fori_loop(0, SLOTS, tally, 0)
    return live, inside // 2 * 2


def choose_slots(counts, offsets, chosen, early):
    live, first = early_slots(counts, offsets)

    def pick(k, state):
        seen, size = state
        inner = is_inside(offsets, k)
        is_early = inner & (seen < first)
        chosen[size] = k
        take = (is_early == early) & (k < live)
        seen = seen + jnp.where(inner, 1, 0)
        return seen, size + jnp.where(take, 1, 0)

    _, size = lax.fori_loop(0, SLOTS, pick, (0, 0))
    return size


def slot_work(k, out_slot, scale, offsets, extended, amplitudes, probe, tables, patch_grads, probe_total):
    forward, inverse = tables
    n = PATCH
    row = offsets[0, 0, 0, k] + HALF
    col = offsets[0, 0, 1, k] + PATCH
    block = col // n
    lead = col - block * n
    turn = jnp.where(lead == 0, 0, n - lead)
    lane = lane_iota(n)
    parts = []
    for p in range(2):
        a = pltpu.roll(extended[p, block, pl.ds(row, n), :], turn, 1)
        b = pltpu.roll(extended[p, block + 1, pl.ds(row, n), :], turn, 1)
        parts.append(jnp.where(lane < n - lead, a, b))
    obj_r, obj_i = parts
    waves = []
    for m in range(MODES):
        pr, pi = probe[m, 0], probe[m, 1]
        waves.append(jnp.concatenate([pr * obj_r - pi * obj_i, pr * obj_i + pi * obj_r], 1))
    far = left_dft(inverse, to_cols(right_dft(jnp.concatenate(waves, 0), forward)))
    power = far * far
    power = power[:n] + power[n:]
    intensity = power[:, :n] + power[:, n : 2 * n] + power[:, 2 * n : 3 * n] + power[:, 3 * n :]
    measured = amplitudes[k]
    residual = (intensity - measured * measured) * scale
    weighted = far * jnp.concatenate([jnp.concatenate([residual] * MODES, 1)] * 2, 0)
    back = right_dft(to_rows(left_dft(forward, weighted)), inverse)
    total_r = total_i = None
    for m in range(MODES):
        gr, gi = back[m * n : (m + 1) * n, :n], back[m * n : (m + 1) * n, n:]
        pr, pi = probe[m, 0], probe[m, 1]
        tr, ti = pr * gr + pi * gi, pr * gi - pi * gr
        total_r, total_i = (tr, ti) if m == 0 else (total_r + tr, total_i + ti)
        probe_total[m, 0] += obj_r * gr + obj_i * gi
        probe_total[m, 1] += obj_r * gi - obj_i * gr
    patch_grads[out_slot, 0] = total_r
    patch_grads[out_slot, 1] = total_i


def tile_copies(tile, extended, sem):
    return [
        pltpu.make_async_copy(
            tile.at[:, :, pl.ds(b * PATCH, PATCH)], extended.at[:, b + 1, pl.ds(HALF, TILE), :], sem
        )
        for b in range(TILE // PATCH)
    ]


def run_slots(early, counts, offsets, amps, patch_grads, probe_in, probe_total, scratch, copies, others=()):
    extended, measured, probe, grads, forward, inverse, chosen, sem, out_sems = scratch
    copies = copies + [pltpu.make_async_copy(amps, measured, sem), pltpu.make_async_copy(probe_in, probe, sem)]
    for c in copies:
        c.start()
    size = choose_slots(counts, offsets, chosen, early)
    for c in [*copies, *others]:
        c.wait()

    def step(first, count):
        for u in range(count):
            i = first + u
            on = i < size
            k = jnp.where(on, chosen[jnp.minimum(i, SLOTS - 1)], 0)
            out = jnp.where(on, k, SLOTS)
            scale = jnp.where(on, 2.0, 0.0)
            slot_work(k, out, scale, offsets, extended, measured, probe, (forward, inverse), grads, probe_total)
        for u in range(count):
            i = first + u

            @pl.when(i < size)
            def _():
                k = chosen[i]
                pltpu.make_async_copy(grads.at[k], patch_grads.at[k], out_sems.at[k]).start()

    whole = size // GROUP * GROUP

    def group(j, carry):
        step(j * GROUP, GROUP)
        return carry

    def pair(j, carry):
        step(whole + j * 2, 2)
        return carry

    lax.fori_loop(0, size // GROUP, group, 0)
    lax.fori_loop(0, (size - whole + 1) // 2, pair, 0)

    def finish(i, carry):
        k = chosen[i]
        pltpu.make_async_copy(grads.at[k], patch_grads.at[k], out_sems.at[k]).wait()
        return carry

    lax.fori_loop(0, size, finish, 0)


def early_kernel(counts, offsets, tile, amps, probe, forward, inverse, patch_grads, probe_total, *scratch):
    extended, sem = scratch[0], scratch[-2]
    copies = tile_copies(tile, extended, sem) + [
        pltpu.make_async_copy(forward, scratch[4], sem),
        pltpu.make_async_copy(inverse, scratch[5], sem),
    ]
    probe_total[...] = jnp.zeros_like(probe_total)
    run_slots(True, counts, offsets, amps, patch_grads, probe, probe_total, scratch, copies)


def late_kernel(
    counts, offsets, sides, tile, rows_a, rows_b, amps, probe, forward, inverse, cols_a, cols_b, corners_a, corners_b,
    probe_before, patch_grads, probe_kept, probe_sent, probe_total, *scratch
):
    extended, side_sem, sem = scratch[0], scratch[-3], scratch[-2]
    scratch = scratch[:-3] + scratch[-2:]
    copies = tile_copies(tile, extended, sem) + [
        pltpu.make_async_copy(forward, scratch[4], sem),
        pltpu.make_async_copy(inverse, scratch[5], sem),
    ]
    even_row, even_col = sides[0] == 0, sides[1] == 0

    def strip_copies(above, below):
        return [
            pltpu.make_async_copy(
                source.at[:, :, pl.ds(b * PATCH, PATCH)], extended.at[:, b + 1, pl.ds(top, HALF), :], side_sem
            )
            for source, top in ((above, 0), (below, HALF + TILE))
            for b in range(TILE // PATCH)
        ]

    def start(above, below):
        for c in strip_copies(above, below):
            c.start()

    @pl.when(even_row)
    def _():
        start(rows_b, rows_a)

    @pl.when(jnp.logical_not(even_row))
    def _():
        start(rows_a, rows_b)

    probe_total[...] = probe_before[...]

    def columns(left, right, left_corners, right_corners):
        for rows, l, r in (
            (pl.ds(HALF, TILE), left[...], right[...]),
            (pl.ds(0, HALF), left_corners[:HALF, :], right_corners[:HALF, :]),
            (pl.ds(HALF + TILE, HALF), left_corners[HALF:, :], right_corners[HALF:, :]),
        ):
            extended[0, 0, rows, :] = pltpu.roll(l, HALF, 1)
            extended[1, 0, rows, :] = l
            extended[0, BLOCKS - 1, rows, :] = r
            extended[1, BLOCKS - 1, rows, :] = pltpu.roll(r, HALF, 1)

    @pl.when(even_col)
    def _():
        columns(cols_b, cols_a, corners_b, corners_a)

    @pl.when(jnp.logical_not(even_col))
    def _():
        columns(cols_a, cols_b, corners_a, corners_b)

    run_slots(
        False, counts, offsets, amps, patch_grads, probe, probe_total, scratch, copies, strip_copies(rows_a, rows_b)
    )
    half = MODES // 2
    put_by_side(even_col, probe_kept, probe_sent, probe_total[:half], probe_total[half:])


def put_by_side(even, a, b, after, before):
    @pl.when(even)
    def _():
        a[...] = after
        b[...] = before

    @pl.when(jnp.logical_not(even))
    def _():
        a[...] = before
        b[...] = after


def pack_kernel(sides, first, last, cols_a, cols_b):
    low = lane_iota(TILE) < HALF
    put_by_side(
        sides[1] == 0,
        cols_a,
        cols_b,
        jnp.where(low, pltpu.roll(last[0], HALF, 1), last[1]),
        jnp.where(low, first[0], pltpu.roll(first[1], HALF, 1)),
    )


def pack_corners_kernel(sides, rows_a, rows_b, corners_a, corners_b, first, last, sem):
    even_row = sides[0] == 0
    copies = []
    for i, source in enumerate((rows_a, rows_b)):
        copies.append(pltpu.make_async_copy(source.at[:, :, pl.ds(0, PATCH)], first.at[i], sem))
        copies.append(pltpu.make_async_copy(source.at[:, :, pl.ds(TILE - PATCH, PATCH)], last.at[i], sem))
    for c in copies:
        c.start()
    for c in copies:
        c.wait()
    low = lane_iota(HALF) < HALF
    for i in range(2):
        l = jnp.where(even_row, first[1 - i], first[i])
        r = jnp.where(even_row, last[1 - i], last[i])
        rows = pl.ds(i * HALF, HALF)
        put_by_side(
            sides[1] == 0,
            corners_a.at[rows, :],
            corners_b.at[rows, :],
            jnp.where(low, pltpu.roll(r[0], HALF, 1), r[1]),
            jnp.where(low, l[0], pltpu.roll(l[1], HALF, 1)),
        )


def deposit_kernel(
    counts, offsets, sides, early_grads, late_grads, inner, top, bottom, cols_a, cols_b, total, held, sems, out_sem
):
    n = PATCH
    live, first = early_slots(counts, offsets)

    def fetch(k, seen):
        inside = is_inside(offsets, k)
        is_early = inside & (seen < first)

        @pl.when(is_early)
        def _():
            pltpu.make_async_copy(early_grads.at[k], held.at[k], sems.at[k]).start()

        @pl.when(jnp.logical_not(is_early))
        def _():
            pltpu.make_async_copy(late_grads.at[k], held.at[k], sems.at[k]).start()

        return seen + jnp.where(inside, 1, 0)

    lax.fori_loop(0, live, fetch, 0)
    total[...] = jnp.zeros_like(total)
    lane = lane_iota(n)

    def turned(k):
        lead = (offsets[0, 0, 1, k] + n) % n
        pltpu.make_async_copy(early_grads.at[k], held.at[k], sems.at[k]).wait()
        return [pltpu.roll(held[k, p], lead, 1) for p in range(2)]

    def add(k, parts):
        row = offsets[0, 0, 0, k] + HALF
        col = offsets[0, 0, 1, k] + n
        block = col // n
        lead = col - block * n
        rows = pl.ds(row, n)
        old = [[total[p, block + i, rows, :] for i in range(2)] for p in range(2)]
        for p in range(2):
            total[p, block, rows, :] = old[p][0] + jnp.where(lane >= lead, parts[p], 0.0)
            total[p, block + 1, rows, :] = old[p][1] + jnp.where(lane < lead, parts[p], 0.0)

    def add_two(j, carry):
        one, two = turned(2 * j), turned(2 * j + 1)
        add(2 * j, one)
        add(2 * j + 1, two)
        return carry

    lax.fori_loop(0, live // 2, add_two, 0)

    @pl.when(live % 2 == 1)
    def _():
        add(live - 1, turned(live - 1))

    copies = []
    for start, rows, out in ((0, HALF, top), (HALF, TILE, inner), (HALF + TILE, HALF, bottom)):
        for b in range(TILE // n):
            near, far = total.at[:, b + 1, pl.ds(start, rows), :], out.at[:, :, pl.ds(b * n, n)]
            copies.append(pltpu.make_async_copy(near, far, out_sem))
    for c in copies:
        c.start()
    low = lane_iota(EXT) < HALF
    put_by_side(
        sides[1] == 0,
        cols_a,
        cols_b,
        jnp.where(low, total[0, BLOCKS - 1], pltpu.roll(total[1, BLOCKS - 1], HALF, 1)),
        jnp.where(low, pltpu.roll(total[0, 0], HALF, 1), total[1, 0]),
    )
    for c in copies:
        c.wait()


def side_terms(even_col, a, b):
    low = lane_iota(a.shape[0]) < HALF
    from_left, from_right = jnp.where(even_col, b, a), jnp.where(even_col, a, b)
    first = (jnp.where(low, from_left, 0.0), jnp.where(low, pltpu.roll(from_left, HALF, 1), 0.0))
    last = (jnp.where(low, 0.0, pltpu.roll(from_right, HALF, 1)), jnp.where(low, 0.0, from_right))
    return first, last


def edges_kernel(sides, top, bottom, cols_a, cols_b, rows_a, rows_b):
    end = TILE - PATCH
    sent = []
    for part, rows in ((top, slice(0, HALF)), (bottom, slice(HALF + TILE, EXT))):
        first, last = side_terms(sides[1] == 0, cols_a[rows, :], cols_b[rows, :])
        sent.append(
            [
                jnp.concatenate([part[p, :, :PATCH] + first[p], part[p, :, PATCH:end], part[p, :, end:] + last[p]], 1)
                for p in range(2)
            ]
        )
    for p in range(2):
        put_by_side(sides[0] == 0, rows_a.at[p], rows_b.at[p], sent[1][p], sent[0][p])


def merge_kernel(sides, inner, cols_a, cols_b, rows_a, rows_b, out, left, right, top, bottom, sems):
    end = TILE - PATCH
    regions = (
        (out.at[:, :, pl.ds(0, PATCH)], left),
        (out.at[:, :, pl.ds(end, PATCH)], right),
        (out.at[:, pl.ds(0, HALF), pl.ds(PATCH, TILE - 2 * PATCH)], top),
        (out.at[:, pl.ds(TILE - HALF, HALF), pl.ds(PATCH, TILE - 2 * PATCH)], bottom),
    )
    loads = [pltpu.make_async_copy(far, near, sems.at[i]) for i, (far, near) in enumerate(regions)]
    for c in loads:
        c.start()
    a, b = rows_a[...], rows_b[...]
    above, below = jnp.where(sides[0] == 0, b, a), jnp.where(sides[0] == 0, a, b)
    own = slice(HALF, HALF + TILE)
    terms = side_terms(sides[1] == 0, cols_a[own, :], cols_b[own, :])
    for c in loads:
        c.wait()
    middle = slice(PATCH, end)
    for p in range(2):
        for near, term, lanes in ((left, terms[0][p], slice(0, PATCH)), (right, terms[1][p], slice(end, TILE))):
            near[p] += term
            near[p, :HALF, :] += above[p, :, lanes]
            near[p, TILE - HALF :, :] += below[p, :, lanes]
        top[p] += above[p, :, middle]
        bottom[p] += below[p, :, middle]
    stores = [pltpu.make_async_copy(near, far, sems.at[i]) for i, (far, near) in enumerate(regions)]
    for c in stores:
        c.start()
    for c in stores:
        c.wait()


VMEM = pl.BlockSpec(memory_space=pltpu.VMEM)
SMEM = pl.BlockSpec(memory_space=pltpu.SMEM)
HBM = pl.BlockSpec(memory_space=pltpu.HBM)


def call(kernel, in_specs, out_specs, out_shapes, scratch, *args, aliases=None, limit=62):
    return pl.pallas_call(
        kernel,
        in_specs=in_specs,
        out_specs=out_specs,
        out_shape=[jax.ShapeDtypeStruct(s, jnp.float32) for s in out_shapes],
        scratch_shapes=scratch,
        input_output_aliases=aliases or {},
        compiler_params=pltpu.CompilerParams(vmem_limit_bytes=limit * 2**20),
    )(*args)


def swap(value, axes, size, first):
    pairs = [(i, i + 1) for i in range(first, size - 1, 2)]
    return lax.ppermute(value, axes, pairs + [(j, i) for i, j in pairs])


def double(x, axis):
    other, me = swap(x, axis, 2, 0), lax.axis_index(axis)
    return jnp.where(me == 0, jnp.concatenate([x, other], 0), jnp.concatenate([other, x], 0))


def deal(x, axes, sizes):
    count = math.prod(sizes[a] for a in axes)
    return lax.all_to_all(x.reshape(count, -1, PATCH), axes, 0, 0, tiled=True)


def spread(x, axes, sizes):
    count = math.prod(sizes[a] for a in axes)
    return lax.all_to_all(jnp.broadcast_to(x[None], (count, *x.shape)), axes, 0, 0, tiled=True)


def per_device(sizes, tile, probe, amplitudes, offsets, counts):
    rows, cols = sizes["zh"] * sizes["x"], sizes["y"] * sizes["zl"] * sizes["core"]
    forward, inverse = [jnp.asarray(t) for t in dft_tables(PATCH)]
    offsets = offsets.transpose(0, 1, 3, 2)
    amps = amplitudes.reshape(SLOTS, PATCH, PATCH)
    odd_row, odd_col = lax.axis_index(ROW) % 2, lax.axis_index(COL) % 2
    sides = jnp.stack([odd_row, odd_col]).astype(jnp.int32)
    wide = 2 * PATCH
    slot_scratch = [
        pltpu.VMEM((2, BLOCKS, EXT, PATCH), jnp.float32),
        pltpu.VMEM((SLOTS, PATCH, PATCH), jnp.float32),
        pltpu.VMEM((MODES, 2, PATCH, PATCH), jnp.float32),
        pltpu.VMEM((SLOTS + 1, 2, PATCH, PATCH), jnp.float32),
        pltpu.VMEM((2, wide, wide), jnp.bfloat16),
        pltpu.VMEM((2, wide, wide), jnp.bfloat16),
        pltpu.SMEM((SLOTS + 1,), jnp.int32),
        pltpu.SemaphoreType.DMA,
        pltpu.SemaphoreType.DMA((SLOTS,)),
    ]
    grads_shape, probe_shape = (SLOTS, 2, PATCH, PATCH), (MODES, 2, PATCH, PATCH)
    strip, column = (2, HALF, TILE), (TILE, PATCH)
    block = pltpu.VMEM((2, TILE, PATCH), jnp.float32)
    low, high = 0, TILE - HALF
    after = lax.dynamic_slice_in_dim(tile, jnp.where(odd_row == 0, high, low), HALF, 1)
    before = lax.dynamic_slice_in_dim(tile, jnp.where(odd_row == 0, low, high), HALF, 1)
    rows_b = swap(before, ROW, rows, 1)
    rows_a = swap(after, ROW, rows, 0)
    cols_a, cols_b = call(
        pack_kernel, [SMEM] + [VMEM] * 2, [VMEM] * 2, [column] * 2, [],
        sides, tile[:, :, :PATCH], tile[:, :, TILE - PATCH :], limit=16
    )
    cols_b = swap(cols_b, COL, cols, 1)
    cols_a = swap(cols_a, COL, cols, 0)
    early_grads, probe_early = call(
        early_kernel, [SMEM] * 2 + [HBM] * 5, [HBM, VMEM], [grads_shape, probe_shape], slot_scratch,
        counts, offsets, tile, amps, probe, forward, inverse
    )
    rows_a, rows_b, probe_early = lax.optimization_barrier((rows_a, rows_b, probe_early))
    piece = pltpu.VMEM((2, 2, HALF, PATCH), jnp.float32)
    corners_a, corners_b = call(
        pack_corners_kernel, [SMEM] + [HBM] * 2, [VMEM] * 2, [(PATCH, PATCH)] * 2, [piece, piece, pltpu.SemaphoreType.DMA],
        sides, rows_a, rows_b, limit=16
    )
    corners_b = swap(corners_b, COL, cols, 1)
    corners_a = swap(corners_a, COL, cols, 0)
    half_shape = (MODES // 2, 2, PATCH, PATCH)
    late_scratch = [pltpu.VMEM(probe_shape, jnp.float32)] + slot_scratch[:-2] + [pltpu.SemaphoreType.DMA] + slot_scratch[-2:]
    late_grads, probe_kept, probe_sent = call(
        late_kernel, [SMEM] * 3 + [HBM] * 7 + [VMEM] * 5, [HBM, VMEM, VMEM], [grads_shape, half_shape, half_shape], late_scratch,
        counts, offsets, sides, tile, rows_a, rows_b, amps, probe, forward, inverse, cols_a, cols_b, corners_a, corners_b, probe_early
    )

    sums = (probe_kept + swap(probe_sent, "core", 2, 0)).reshape(-1, PATCH)
    inner, top, bottom, cols_a, cols_b = call(
        deposit_kernel, [SMEM] * 3 + [HBM] * 2, [HBM] * 3 + [VMEM] * 2,
        [(2, TILE, TILE), strip, strip, (EXT, PATCH), (EXT, PATCH)],
        [
            pltpu.VMEM((2, BLOCKS, EXT, PATCH), jnp.float32),
            pltpu.VMEM(grads_shape, jnp.float32),
            pltpu.SemaphoreType.DMA((SLOTS,)),
            pltpu.SemaphoreType.DMA,
        ],
        counts, offsets, sides, early_grads, late_grads
    )
    cols_b = swap(cols_b, COL, cols, 1)
    cols_a = swap(cols_a, COL, cols, 0)
    plane, line = ("x", "y"), ("zh", "zl")
    sums = jnp.sum(deal(sums, plane, sizes), 0)
    rows_a, rows_b = call(
        edges_kernel, [SMEM] + [VMEM] * 4, [VMEM] * 2, [strip] * 2, [], sides, top, bottom, cols_a, cols_b, limit=16
    )
    sums = jnp.sum(spread(sums, line, sizes), 0)
    rows_b = swap(rows_b, ROW, rows, 1)
    rows_a = swap(rows_a, ROW, rows, 0)
    sums = spread(sums, plane, sizes).reshape(-1, PATCH)
    sums, rows_a, rows_b = lax.optimization_barrier((sums, rows_a, rows_b))
    end = pltpu.VMEM((2, HALF, TILE - 2 * PATCH), jnp.float32)
    (object_grad,) = call(
        merge_kernel, [SMEM, HBM] + [VMEM] * 4, [HBM], [(2, TILE, TILE)],
        [block, block, end, end, pltpu.SemaphoreType.DMA((4,))],
        sides, inner, cols_a, cols_b, rows_a, rows_b, aliases={1: 0}, limit=16
    )
    factor = 1.0 / math.sqrt(rows * cols * SLOTS)
    probe_grad = (double(sums, "core") * factor).reshape(probe_shape)
    return object_grad, probe_grad


def solution(mesh):
    sizes = {"zh": 4, "x": 4, "y": 4, "zl": 2, "core": 2}
    fine = Mesh(mesh.devices.reshape(tuple(sizes.values())), tuple(sizes))
    return jax.shard_map(
        functools.partial(per_device, sizes),
        mesh=fine,
        in_specs=(P(None, ROW, COL), P(), P(ROW, COL), P(ROW, COL), P(ROW, COL)),
        out_specs=(P(None, ROW, COL), P()),
        check_vma=False,
    )
```

```python
import functools
import math

import jax
import jax.numpy as jnp
import ml_dtypes
import numpy as np
from jax import lax
from jax.experimental import pallas as pl
from jax.experimental.pallas import tpu as pltpu
from jax.sharding import Mesh
from jax.sharding import PartitionSpec as P

PATCH = 128
MODES = 4
TILE = 512
SLOTS = 16
HALF = 64
EXT = TILE + 2 * HALF
BLOCKS = 6
GROUP = 4

ROW = ("zh", "x")
COL = ("y", "zl", "core")


def split_table(table):
    high = table.astype(np.float32).astype(ml_dtypes.bfloat16)
    low = (table - high.astype(np.float64)).astype(np.float32).astype(ml_dtypes.bfloat16)
    return high, low


def dft_tables(n):
    i = np.arange(n)
    angles = (np.outer(i, i) % n) * (2 * math.pi / n)
    cos, sin = np.cos(angles) / math.sqrt(n), -np.sin(angles) / math.sqrt(n)
    forward = np.block([[cos, sin], [-sin, cos]])
    fh, fl = split_table(forward)
    ih, il = split_table(forward.T)
    return np.stack([fh, fl]), np.stack([ih, il])


def split(x):
    high = x.astype(jnp.bfloat16)
    return high, (x - high.astype(jnp.float32)).astype(jnp.bfloat16)


def dot(a, b):
    return jnp.dot(a, b, preferred_element_type=jnp.float32)


def right_dft(x, table):
    high, low = split(x)
    return dot(high, table[0]) + dot(low, table[0]) + dot(high, table[1])


def left_dft(table, x):
    high, low = split(x)
    return dot(table[0], high) + dot(table[1], high) + dot(table[0], low)


def to_cols(y):
    n = PATCH
    return jnp.concatenate(
        [jnp.concatenate([y[m * n : (m + 1) * n, p * n : (p + 1) * n] for m in range(MODES)], 1) for p in range(2)], 0
    )


def to_rows(z):
    n = PATCH
    return jnp.concatenate(
        [jnp.concatenate([z[p * n : (p + 1) * n, m * n : (m + 1) * n] for p in range(2)], 1) for m in range(MODES)], 0
    )


def lane_iota(rows):
    return lax.broadcasted_iota(jnp.int32, (rows, PATCH), 1)


def is_inside(offsets, k):
    r, c = offsets[0, 0, 0, k], offsets[0, 0, 1, k]
    top = TILE - PATCH
    return (r >= 0) & (r <= top) & (c >= 0) & (c <= top)


def early_slots(counts, offsets):
    live = counts[0, 0]

    def tally(k, total):
        return total + jnp.where(is_inside(offsets, k) & (k < live), 1, 0)

    inside = lax.fori_loop(0, SLOTS, tally, 0)
    return live, inside // 2 * 2


def choose_slots(counts, offsets, chosen, early):
    live, first = early_slots(counts, offsets)

    def pick(k, state):
        seen, size = state
        inner = is_inside(offsets, k)
        is_early = inner & (seen < first)
        chosen[size] = k
        take = (is_early == early) & (k < live)
        seen = seen + jnp.where(inner, 1, 0)
        return seen, size + jnp.where(take, 1, 0)

    _, size = lax.fori_loop(0, SLOTS, pick, (0, 0))
    return size


def slot_work(k, out_slot, scale, offsets, extended, amplitudes, probe, tables, patch_grads, probe_total):
    forward, inverse = tables
    n = PATCH
    row = offsets[0, 0, 0, k] + HALF
    col = offsets[0, 0, 1, k] + PATCH
    block = col // n
    lead = col - block * n
    turn = jnp.where(lead == 0, 0, n - lead)
    lane = lane_iota(n)
    parts = []
    for p in range(2):
        a = pltpu.roll(extended[p, block, pl.ds(row, n), :], turn, 1)
        b = pltpu.roll(extended[p, block + 1, pl.ds(row, n), :], turn, 1)
        parts.append(jnp.where(lane < n - lead, a, b))
    obj_r, obj_i = parts
    waves = []
    for m in range(MODES):
        pr, pi = probe[m, 0], probe[m, 1]
        waves.append(jnp.concatenate([pr * obj_r - pi * obj_i, pr * obj_i + pi * obj_r], 1))
    far = left_dft(inverse, to_cols(right_dft(jnp.concatenate(waves, 0), forward)))
    power = far * far
    power = power[:n] + power[n:]
    intensity = power[:, :n] + power[:, n : 2 * n] + power[:, 2 * n : 3 * n] + power[:, 3 * n :]
    measured = amplitudes[k]
    residual = (intensity - measured * measured) * scale
    weighted = far * jnp.concatenate([jnp.concatenate([residual] * MODES, 1)] * 2, 0)
    back = right_dft(to_rows(left_dft(forward, weighted)), inverse)
    total_r = total_i = None
    for m in range(MODES):
        gr, gi = back[m * n : (m + 1) * n, :n], back[m * n : (m + 1) * n, n:]
        pr, pi = probe[m, 0], probe[m, 1]
        tr, ti = pr * gr + pi * gi, pr * gi - pi * gr
        total_r, total_i = (tr, ti) if m == 0 else (total_r + tr, total_i + ti)
        probe_total[m, 0] += obj_r * gr + obj_i * gi
        probe_total[m, 1] += obj_r * gi - obj_i * gr
    patch_grads[out_slot, 0] = total_r
    patch_grads[out_slot, 1] = total_i


def tile_copies(tile, extended, sem):
    return [
        pltpu.make_async_copy(
            tile.at[:, :, pl.ds(b * PATCH, PATCH)], extended.at[:, b + 1, pl.ds(HALF, TILE), :], sem
        )
        for b in range(TILE // PATCH)
    ]


def run_slots(early, counts, offsets, amps, patch_grads, probe_in, probe_total, scratch, copies, others=()):
    extended, measured, probe, grads, forward, inverse, chosen, sem, out_sems = scratch
    copies = copies + [pltpu.make_async_copy(amps, measured, sem), pltpu.make_async_copy(probe_in, probe, sem)]
    for c in copies:
        c.start()
    size = choose_slots(counts, offsets, chosen, early)
    for c in [*copies, *others]:
        c.wait()

    def step(first, count):
        for u in range(count):
            i = first + u
            on = i < size
            k = jnp.where(on, chosen[jnp.minimum(i, SLOTS - 1)], 0)
            out = jnp.where(on, k, SLOTS)
            scale = jnp.where(on, 2.0, 0.0)
            slot_work(k, out, scale, offsets, extended, measured, probe, (forward, inverse), grads, probe_total)
        for u in range(count):
            i = first + u

            @pl.when(i < size)
            def _():
                k = chosen[i]
                pltpu.make_async_copy(grads.at[k], patch_grads.at[k], out_sems.at[k]).start()

    whole = size // GROUP * GROUP

    def group(j, carry):
        step(j * GROUP, GROUP)
        return carry

    def pair(j, carry):
        step(whole + j * 2, 2)
        return carry

    lax.fori_loop(0, size // GROUP, group, 0)
    lax.fori_loop(0, (size - whole + 1) // 2, pair, 0)

    def finish(i, carry):
        k = chosen[i]
        pltpu.make_async_copy(grads.at[k], patch_grads.at[k], out_sems.at[k]).wait()
        return carry

    lax.fori_loop(0, size, finish, 0)


def early_kernel(counts, offsets, tile, amps, probe, forward, inverse, patch_grads, probe_total, *scratch):
    extended, sem = scratch[0], scratch[-2]
    copies = tile_copies(tile, extended, sem) + [
        pltpu.make_async_copy(forward, scratch[4], sem),
        pltpu.make_async_copy(inverse, scratch[5], sem),
    ]
    probe_total[...] = jnp.zeros_like(probe_total)
    run_slots(True, counts, offsets, amps, patch_grads, probe, probe_total, scratch, copies)


def late_kernel(
    counts, offsets, sides, tile, rows_a, rows_b, amps, probe, forward, inverse, cols_a, cols_b, corners_a, corners_b,
    probe_before, patch_grads, probe_kept, probe_sent, probe_total, *scratch
):
    extended, side_sem, sem = scratch[0], scratch[-3], scratch[-2]
    scratch = scratch[:-3] + scratch[-2:]
    copies = tile_copies(tile, extended, sem) + [
        pltpu.make_async_copy(forward, scratch[4], sem),
        pltpu.make_async_copy(inverse, scratch[5], sem),
    ]
    even_row, even_col = sides[0] == 0, sides[1] == 0

    def strip_copies(above, below):
        return [
            pltpu.make_async_copy(
                source.at[:, :, pl.ds(b * PATCH, PATCH)], extended.at[:, b + 1, pl.ds(top, HALF), :], side_sem
            )
            for source, top in ((above, 0), (below, HALF + TILE))
            for b in range(TILE // PATCH)
        ]

    def start(above, below):
        for c in strip_copies(above, below):
            c.start()

    @pl.when(even_row)
    def _():
        start(rows_b, rows_a)

    @pl.when(jnp.logical_not(even_row))
    def _():
        start(rows_a, rows_b)

    probe_total[...] = probe_before[...]

    def columns(left, right, left_corners, right_corners):
        for rows, l, r in (
            (pl.ds(HALF, TILE), left[...], right[...]),
            (pl.ds(0, HALF), left_corners[:HALF, :], right_corners[:HALF, :]),
            (pl.ds(HALF + TILE, HALF), left_corners[HALF:, :], right_corners[HALF:, :]),
        ):
            extended[0, 0, rows, :] = pltpu.roll(l, HALF, 1)
            extended[1, 0, rows, :] = l
            extended[0, BLOCKS - 1, rows, :] = r
            extended[1, BLOCKS - 1, rows, :] = pltpu.roll(r, HALF, 1)

    @pl.when(even_col)
    def _():
        columns(cols_b, cols_a, corners_b, corners_a)

    @pl.when(jnp.logical_not(even_col))
    def _():
        columns(cols_a, cols_b, corners_a, corners_b)

    run_slots(
        False, counts, offsets, amps, patch_grads, probe, probe_total, scratch, copies, strip_copies(rows_a, rows_b)
    )
    half = MODES // 2
    put_by_side(even_col, probe_kept, probe_sent, probe_total[:half], probe_total[half:])


def put_by_side(even, a, b, after, before):
    @pl.when(even)
    def _():
        a[...] = after
        b[...] = before

    @pl.when(jnp.logical_not(even))
    def _():
        a[...] = before
        b[...] = after


def pack_kernel(sides, tile, cols_a, cols_b, first, last, sem):
    copies = [
        pltpu.make_async_copy(tile.at[:, :, pl.ds(0, PATCH)], first, sem),
        pltpu.make_async_copy(tile.at[:, :, pl.ds(TILE - PATCH, PATCH)], last, sem),
    ]
    for c in copies:
        c.start()
    for c in copies:
        c.wait()
    low = lane_iota(TILE) < HALF
    put_by_side(
        sides[1] == 0,
        cols_a,
        cols_b,
        jnp.where(low, pltpu.roll(last[0], HALF, 1), last[1]),
        jnp.where(low, first[0], pltpu.roll(first[1], HALF, 1)),
    )


def pack_corners_kernel(sides, rows_a, rows_b, corners_a, corners_b, first, last, sem):
    even_row = sides[0] == 0
    copies = []
    for i, source in enumerate((rows_a, rows_b)):
        copies.append(pltpu.make_async_copy(source.at[:, :, pl.ds(0, PATCH)], first.at[i], sem))
        copies.append(pltpu.make_async_copy(source.at[:, :, pl.ds(TILE - PATCH, PATCH)], last.at[i], sem))
    for c in copies:
        c.start()
    for c in copies:
        c.wait()
    low = lane_iota(HALF) < HALF
    for i in range(2):
        l = jnp.where(even_row, first[1 - i], first[i])
        r = jnp.where(even_row, last[1 - i], last[i])
        rows = pl.ds(i * HALF, HALF)
        put_by_side(
            sides[1] == 0,
            corners_a.at[rows, :],
            corners_b.at[rows, :],
            jnp.where(low, pltpu.roll(r[0], HALF, 1), r[1]),
            jnp.where(low, l[0], pltpu.roll(l[1], HALF, 1)),
        )


def deposit_kernel(
    counts, offsets, sides, early_grads, late_grads, inner, top, bottom, cols_a, cols_b, total, held, sems, out_sem
):
    n = PATCH
    live, first = early_slots(counts, offsets)

    def fetch(k, seen):
        inside = is_inside(offsets, k)
        is_early = inside & (seen < first)

        @pl.when(is_early)
        def _():
            pltpu.make_async_copy(early_grads.at[k], held.at[k], sems.at[k]).start()

        @pl.when(jnp.logical_not(is_early))
        def _():
            pltpu.make_async_copy(late_grads.at[k], held.at[k], sems.at[k]).start()

        return seen + jnp.where(inside, 1, 0)

    lax.fori_loop(0, live, fetch, 0)
    total[...] = jnp.zeros_like(total)
    lane = lane_iota(n)

    def turned(k):
        lead = (offsets[0, 0, 1, k] + n) % n
        pltpu.make_async_copy(early_grads.at[k], held.at[k], sems.at[k]).wait()
        return [pltpu.roll(held[k, p], lead, 1) for p in range(2)]

    def add(k, parts):
        row = offsets[0, 0, 0, k] + HALF
        col = offsets[0, 0, 1, k] + n
        block = col // n
        lead = col - block * n
        rows = pl.ds(row, n)
        old = [[total[p, block + i, rows, :] for i in range(2)] for p in range(2)]
        for p in range(2):
            total[p, block, rows, :] = old[p][0] + jnp.where(lane >= lead, parts[p], 0.0)
            total[p, block + 1, rows, :] = old[p][1] + jnp.where(lane < lead, parts[p], 0.0)

    def add_two(j, carry):
        one, two = turned(2 * j), turned(2 * j + 1)
        add(2 * j, one)
        add(2 * j + 1, two)
        return carry

    lax.fori_loop(0, live // 2, add_two, 0)

    @pl.when(live % 2 == 1)
    def _():
        add(live - 1, turned(live - 1))

    copies = []
    for start, rows, out in ((0, HALF, top), (HALF, TILE, inner), (HALF + TILE, HALF, bottom)):
        for b in range(TILE // n):
            near, far = total.at[:, b + 1, pl.ds(start, rows), :], out.at[:, :, pl.ds(b * n, n)]
            copies.append(pltpu.make_async_copy(near, far, out_sem))
    for c in copies:
        c.start()
    low = lane_iota(EXT) < HALF
    put_by_side(
        sides[1] == 0,
        cols_a,
        cols_b,
        jnp.where(low, total[0, BLOCKS - 1], pltpu.roll(total[1, BLOCKS - 1], HALF, 1)),
        jnp.where(low, pltpu.roll(total[0, 0], HALF, 1), total[1, 0]),
    )
    for c in copies:
        c.wait()


def side_terms(even_col, a, b):
    low = lane_iota(a.shape[0]) < HALF
    from_left, from_right = jnp.where(even_col, b, a), jnp.where(even_col, a, b)
    first = (jnp.where(low, from_left, 0.0), jnp.where(low, pltpu.roll(from_left, HALF, 1), 0.0))
    last = (jnp.where(low, 0.0, pltpu.roll(from_right, HALF, 1)), jnp.where(low, 0.0, from_right))
    return first, last


def edges_kernel(sides, top, bottom, cols_a, cols_b, rows_a, rows_b):
    end = TILE - PATCH
    sent = []
    for part, rows in ((top, slice(0, HALF)), (bottom, slice(HALF + TILE, EXT))):
        first, last = side_terms(sides[1] == 0, cols_a[rows, :], cols_b[rows, :])
        sent.append(
            [
                jnp.concatenate([part[p, :, :PATCH] + first[p], part[p, :, PATCH:end], part[p, :, end:] + last[p]], 1)
                for p in range(2)
            ]
        )
    for p in range(2):
        put_by_side(sides[0] == 0, rows_a.at[p], rows_b.at[p], sent[1][p], sent[0][p])


def merge_kernel(sides, inner, cols_a, cols_b, rows_a, rows_b, out, left, right, top, bottom, sems):
    end = TILE - PATCH
    regions = (
        (out.at[:, :, pl.ds(0, PATCH)], left),
        (out.at[:, :, pl.ds(end, PATCH)], right),
        (out.at[:, pl.ds(0, HALF), pl.ds(PATCH, TILE - 2 * PATCH)], top),
        (out.at[:, pl.ds(TILE - HALF, HALF), pl.ds(PATCH, TILE - 2 * PATCH)], bottom),
    )
    loads = [pltpu.make_async_copy(far, near, sems.at[i]) for i, (far, near) in enumerate(regions)]
    for c in loads:
        c.start()
    a, b = rows_a[...], rows_b[...]
    above, below = jnp.where(sides[0] == 0, b, a), jnp.where(sides[0] == 0, a, b)
    own = slice(HALF, HALF + TILE)
    terms = side_terms(sides[1] == 0, cols_a[own, :], cols_b[own, :])
    for c in loads:
        c.wait()
    middle = slice(PATCH, end)
    for p in range(2):
        for near, term, lanes in ((left, terms[0][p], slice(0, PATCH)), (right, terms[1][p], slice(end, TILE))):
            near[p] += term
            near[p, :HALF, :] += above[p, :, lanes]
            near[p, TILE - HALF :, :] += below[p, :, lanes]
        top[p] += above[p, :, middle]
        bottom[p] += below[p, :, middle]
    stores = [pltpu.make_async_copy(near, far, sems.at[i]) for i, (far, near) in enumerate(regions)]
    for c in stores:
        c.start()
    for c in stores:
        c.wait()


VMEM = pl.BlockSpec(memory_space=pltpu.VMEM)
SMEM = pl.BlockSpec(memory_space=pltpu.SMEM)
HBM = pl.BlockSpec(memory_space=pltpu.HBM)


def call(kernel, in_specs, out_specs, out_shapes, scratch, *args, aliases=None, limit=62):
    return pl.pallas_call(
        kernel,
        in_specs=in_specs,
        out_specs=out_specs,
        out_shape=[jax.ShapeDtypeStruct(s, jnp.float32) for s in out_shapes],
        scratch_shapes=scratch,
        input_output_aliases=aliases or {},
        compiler_params=pltpu.CompilerParams(vmem_limit_bytes=limit * 2**20),
    )(*args)


def swap(value, axes, size, first):
    pairs = [(i, i + 1) for i in range(first, size - 1, 2)]
    return lax.ppermute(value, axes, pairs + [(j, i) for i, j in pairs])


def double(x, axis):
    other, me = swap(x, axis, 2, 0), lax.axis_index(axis)
    return jnp.where(me == 0, jnp.concatenate([x, other], 0), jnp.concatenate([other, x], 0))


def deal(x, axes, sizes):
    count = math.prod(sizes[a] for a in axes)
    return lax.all_to_all(x.reshape(count, -1, PATCH), axes, 0, 0, tiled=True)


def spread(x, axes, sizes):
    count = math.prod(sizes[a] for a in axes)
    return lax.all_to_all(jnp.broadcast_to(x[None], (count, *x.shape)), axes, 0, 0, tiled=True)


def per_device(sizes, tile, probe, amplitudes, offsets, counts):
    rows, cols = sizes["zh"] * sizes["x"], sizes["y"] * sizes["zl"] * sizes["core"]
    forward, inverse = [jnp.asarray(t) for t in dft_tables(PATCH)]
    offsets = offsets.transpose(0, 1, 3, 2)
    amps = amplitudes.reshape(SLOTS, PATCH, PATCH)
    odd_row, odd_col = lax.axis_index(ROW) % 2, lax.axis_index(COL) % 2
    sides = jnp.stack([odd_row, odd_col]).astype(jnp.int32)
    wide = 2 * PATCH
    slot_scratch = [
        pltpu.VMEM((2, BLOCKS, EXT, PATCH), jnp.float32),
        pltpu.VMEM((SLOTS, PATCH, PATCH), jnp.float32),
        pltpu.VMEM((MODES, 2, PATCH, PATCH), jnp.float32),
        pltpu.VMEM((SLOTS + 1, 2, PATCH, PATCH), jnp.float32),
        pltpu.VMEM((2, wide, wide), jnp.bfloat16),
        pltpu.VMEM((2, wide, wide), jnp.bfloat16),
        pltpu.SMEM((SLOTS + 1,), jnp.int32),
        pltpu.SemaphoreType.DMA,
        pltpu.SemaphoreType.DMA((SLOTS,)),
    ]
    grads_shape, probe_shape = (SLOTS, 2, PATCH, PATCH), (MODES, 2, PATCH, PATCH)
    strip, column = (2, HALF, TILE), (TILE, PATCH)
    block = pltpu.VMEM((2, TILE, PATCH), jnp.float32)
    low, high = 0, TILE - HALF
    after = lax.dynamic_slice_in_dim(tile, jnp.where(odd_row == 0, high, low), HALF, 1)
    before = lax.dynamic_slice_in_dim(tile, jnp.where(odd_row == 0, low, high), HALF, 1)
    rows_b = swap(before, ROW, rows, 1)
    rows_a = swap(after, ROW, rows, 0)
    cols_a, cols_b = call(
        pack_kernel, [SMEM, HBM], [VMEM] * 2, [column] * 2, [block, block, pltpu.SemaphoreType.DMA], sides, tile, limit=16
    )
    cols_b = swap(cols_b, COL, cols, 1)
    cols_a = swap(cols_a, COL, cols, 0)
    early_grads, probe_early = call(
        early_kernel, [SMEM] * 2 + [HBM] * 5, [HBM, VMEM], [grads_shape, probe_shape], slot_scratch,
        counts, offsets, tile, amps, probe, forward, inverse
    )
    rows_a, rows_b, probe_early = lax.optimization_barrier((rows_a, rows_b, probe_early))
    piece = pltpu.VMEM((2, 2, HALF, PATCH), jnp.float32)
    corners_a, corners_b = call(
        pack_corners_kernel, [SMEM] + [HBM] * 2, [VMEM] * 2, [(PATCH, PATCH)] * 2, [piece, piece, pltpu.SemaphoreType.DMA],
        sides, rows_a, rows_b, limit=16
    )
    corners_b = swap(corners_b, COL, cols, 1)
    corners_a = swap(corners_a, COL, cols, 0)
    half_shape = (MODES // 2, 2, PATCH, PATCH)
    late_scratch = [pltpu.VMEM(probe_shape, jnp.float32)] + slot_scratch[:-2] + [pltpu.SemaphoreType.DMA] + slot_scratch[-2:]
    late_grads, probe_kept, probe_sent = call(
        late_kernel, [SMEM] * 3 + [HBM] * 7 + [VMEM] * 5, [HBM, VMEM, VMEM], [grads_shape, half_shape, half_shape], late_scratch,
        counts, offsets, sides, tile, rows_a, rows_b, amps, probe, forward, inverse, cols_a, cols_b, corners_a, corners_b, probe_early
    )

    sums = (probe_kept + swap(probe_sent, "core", 2, 0)).reshape(-1, PATCH)
    inner, top, bottom, cols_a, cols_b = call(
        deposit_kernel, [SMEM] * 3 + [HBM] * 2, [HBM] * 3 + [VMEM] * 2,
        [(2, TILE, TILE), strip, strip, (EXT, PATCH), (EXT, PATCH)],
        [
            pltpu.VMEM((2, BLOCKS, EXT, PATCH), jnp.float32),
            pltpu.VMEM(grads_shape, jnp.float32),
            pltpu.SemaphoreType.DMA((SLOTS,)),
            pltpu.SemaphoreType.DMA,
        ],
        counts, offsets, sides, early_grads, late_grads
    )
    cols_a = swap(cols_a, COL, cols, 0)
    cols_b = swap(cols_b, COL, cols, 1)
    plane, line = ("x", "y"), ("zh", "zl")
    sums = jnp.sum(deal(sums, plane, sizes), 0)
    rows_a, rows_b = call(
        edges_kernel, [SMEM] + [VMEM] * 4, [VMEM] * 2, [strip] * 2, [], sides, top, bottom, cols_a, cols_b, limit=16
    )
    sums = jnp.sum(spread(sums, line, sizes), 0)
    rows_a = swap(rows_a, ROW, rows, 0)
    rows_b = swap(rows_b, ROW, rows, 1)
    sums = spread(sums, plane, sizes).reshape(-1, PATCH)
    sums, rows_a, rows_b = lax.optimization_barrier((sums, rows_a, rows_b))
    end = pltpu.VMEM((2, HALF, TILE - 2 * PATCH), jnp.float32)
    (object_grad,) = call(
        merge_kernel, [SMEM, HBM] + [VMEM] * 4, [HBM], [(2, TILE, TILE)],
        [block, block, end, end, pltpu.SemaphoreType.DMA((4,))],
        sides, inner, cols_a, cols_b, rows_a, rows_b, aliases={1: 0}, limit=16
    )
    factor = 1.0 / math.sqrt(rows * cols * SLOTS)
    probe_grad = (double(sums, "core") * factor).reshape(probe_shape)
    return object_grad, probe_grad


def solution(mesh):
    sizes = {"zh": 4, "x": 4, "y": 4, "zl": 2, "core": 2}
    fine = Mesh(mesh.devices.reshape(tuple(sizes.values())), tuple(sizes))
    return jax.shard_map(
        functools.partial(per_device, sizes),
        mesh=fine,
        in_specs=(P(None, ROW, COL), P(), P(ROW, COL), P(ROW, COL), P(ROW, COL)),
        out_specs=(P(None, ROW, COL), P()),
        check_vma=False,
    )
```
